512 devices in a mesh: slide: 16 (over z_lo, x), tile: 32 (over y, z_hi, core).
Axes of the slice: x: 4, y: 4, z: 16 (z_hi: 4, z_lo: 4; z = z_hi * 4 + z_lo), core: 2. Of those that a mesh axis runs over, the one named last changes fastest.
Arguments:
- tiles: bfloat16 [32768, 16, 1024], P(('slide', 'tile')), parts along dimension 0, may hold values from -6 to 6
- w_reduce: bfloat16 [1024, 256], replicated, may hold values from -0.1875 to 0.1875
- w_expand: bfloat16 [1024, 256], replicated, may hold values from -0.375 to 0.375
- att_tanh: bfloat16 [1024, 256], replicated, may hold values from -0.1875 to 0.1875
- att_gate: bfloat16 [1024, 256], replicated, may hold values from -0.1875 to 0.1875
- att_vector: float32 [256], replicated, may hold values from -0.3 to 0.3
- classifier: float32 [1024, 2], replicated, may hold values from -0.09375 to 0.09375
- tile_counts: int32 [512], P(('slide', 'tile')), parts along dimension 0, may hold values from 1 to 64, 1024 in all
- target_weights: float32 [32], P('slide'), parts along dimension 0, may hold values from 0.1 to 1
Outputs:
- grad_w1: float32 [16384, 256], P(('slide', 'tile')), parts along dimension 0
- grad_w2: float32 [16384, 256], P(('slide', 'tile')), parts along dimension 0
- loss: float32 [16], P('slide'), parts along dimension 0
The draws below stay inside these ranges and needn't reach their ends.
There are 16 independent parts, one for each index of `slide`. The reference program is written for one: setup_inputs(seed, part) draws one part's arguments, and reference() takes and returns one part's arrays. A program takes and returns all parts, laid end to end along the dimension named above; an argument that names none is the same for every part. Nothing has to cross between parts.
Inputs may be any that keep to these rules, and one draw needn't show every extreme that they name: `tile_counts`: per device tile counts sum to exactly 1024 over a slide, and some device holds exactly 64.
All inputs are finite; a program needn't handle non-finite values.
Results may differ from the reference program's by a relative error of at most 0.008.
Values may be sent and summed in bfloat16 or wider, within the bound.
No kernel may reach another device: no remote copies, remote signals or barrier semaphores. Data moves between devices by JAX's collectives and lax.ppermute only.
A program may use at most 64 MiB of HBM per device.

```python
import math
import jax
import jax.numpy as jnp
import numpy as np

CH = 1024
HID = 256
ATT = 256
NCLS = 2
POS = 16
CAP = 64
TILES = 2048
SLIDE_TILE_COUNT = 1024
N_TILE = 32


def shard_levels(own_key, extent, cuts, smallest, high):
    factor_of, own = 1.0, jax.random.fold_in(own_key, 6)
    for dim, shards_of in cuts:
        draws = jnp.exp(jax.random.uniform(jax.random.fold_in(own, dim), (shards_of,), jnp.float32, smallest / len(cuts), high / len(cuts)))
        factor_of = factor_of * jnp.repeat(draws, extent[dim] // shards_of).reshape([-1 if axis == dim else 1 for axis in range(len(extent))])
    return factor_of


def profile(amount, total, most, skew):
    portions = [(1 << 20) // math.isqrt(rank ** skew) + 1 for rank in range(2, amount + 1)]
    surplus, given = total - most - (amount - 1), [1] * (amount - 1)
    while surplus > 0:
        free = [i for i in range(amount - 1) if given[i] < most]
        pool, left = sum([portions[i] for i in free]), surplus
        for i in free:
            extra = min(most - given[i], max(1, left * portions[i] // pool), surplus)
            given[i] = given[i] + extra
            surplus = surplus - extra
    return np.array([most] + given)


def ragged(own_key, number_of, total, most, skew):
    if number_of == 2:
        one = jax.random.randint(own_key, (), max(1, total - most), min(most, total - 1) + 1)
        return jnp.stack([one, total - one])
    lengths = jnp.asarray(profile(number_of, total, most, skew), jnp.int32)
    pairs = (number_of - 1) // 2
    source_of, sink = lengths[1:1 + 2 * pairs:2], lengths[2:2 + 2 * pairs:2]
    margin = jnp.minimum(source_of - 1, most - sink)
    shifted = jax.random.randint(jax.random.fold_in(own_key, 1), (pairs,), 0, 1 << 20) % (margin + 1)
    lengths = lengths.at[1:1 + 2 * pairs:2].set(source_of - shifted).at[2:2 + 2 * pairs:2].set(sink + shifted)
    return lengths[jax.random.permutation(jax.random.fold_in(own_key, 2), number_of)]


def centred(key, dims, width, bound, split=(), held_as=jnp.bfloat16):
    result = width * jax.random.normal(key, dims, jnp.float32)
    if split:
        result = result * shard_levels(key, dims, split, -0.22, 0.18)
    return jnp.clip(result, -bound, bound).astype(held_as)


def setup_inputs(seed: int = 0, part: int = 0) -> dict:
    streams_of = jax.random.split(jax.random.key(seed), 10)
    part_keys = jax.random.split(jax.random.fold_in(streams_of[9], part), 10)
    return {
        "tiles": centred(part_keys[0], (TILES, POS, CH), 1.0, 6.0, ((0, 32),)),
        "w_reduce": centred(streams_of[1], (CH, HID), CH ** -0.5, 0.1875),
        "w_expand": centred(streams_of[2], (CH, HID), HID ** -0.5, 0.375),
        "att_tanh": centred(streams_of[3], (CH, ATT), CH ** -0.5, 0.1875),
        "att_gate": centred(streams_of[4], (CH, ATT), CH ** -0.5, 0.1875),
        "att_vector": jnp.clip(jax.random.uniform(streams_of[5], (ATT,), jnp.float32, -0.3, 0.3), -0.3, 0.3),
        "classifier": centred(streams_of[6], (CH, NCLS), (4 * CH) ** -0.5, 0.09375, (), jnp.float32),
        "tile_counts": ragged(part_keys[7], N_TILE, SLIDE_TILE_COUNT, CAP, 2).astype(jnp.int32),
        "target_weights": jnp.clip(jnp.exp(jax.random.uniform(part_keys[8], (NCLS,), jnp.float32, math.log(0.1), math.log(1.0))), 0.1, 1.0),
    }


def reference(tiles, w_reduce, w_expand, att_tanh, att_gate, att_vector, classifier, tile_counts, target_weights):
    rows = tiles.shape[0]
    index = jnp.arange(rows, dtype=jnp.int32)
    live = ((index % CAP) < tile_counts[index // CAP]).astype(jnp.float32)
    flat = tiles.reshape(rows * POS, CH)
    hidden = jnp.maximum(jnp.dot(flat, w_reduce, preferred_element_type=jnp.float32), 0.0).astype(jnp.bfloat16)
    output = flat.astype(jnp.float32) + jnp.dot(hidden, w_expand.T, preferred_element_type=jnp.float32)
    embed = (jnp.sum(output.reshape(rows, POS, CH), axis=1) / POS).astype(jnp.bfloat16)
    tanh_part = jnp.tanh(jnp.dot(embed, att_tanh, preferred_element_type=jnp.float32))
    gate_part = jax.nn.sigmoid(jnp.dot(embed, att_gate, preferred_element_type=jnp.float32))
    score = jnp.sum(tanh_part * gate_part * att_vector, axis=1)
    weight = live * jnp.exp(score)
    total = jnp.sum(weight)
    embed_float = embed.astype(jnp.float32)
    pooled = jnp.sum(weight[:, None] * embed_float, axis=0) / total
    target_share = target_weights / jnp.sum(target_weights)
    class_scores = jnp.sum(pooled[:, None] * classifier, axis=0)
    log_partition_sum = jnp.log(jnp.sum(jnp.exp(class_scores)))
    loss = log_partition_sum - jnp.sum(class_scores * target_share)
    logit_gradient = SLIDE_TILE_COUNT * (jnp.exp(class_scores - log_partition_sum) - target_share)
    pooled_gradient = jnp.sum(classifier * logit_gradient[None, :], axis=1)
    prob = weight / total
    dscore = prob * (jnp.sum(embed_float * pooled_gradient, axis=1) - jnp.sum(pooled * pooled_gradient))
    dact = dscore[:, None] * att_vector
    dtanh = (dact * gate_part * (1.0 - tanh_part * tanh_part)).astype(jnp.bfloat16)
    dgate = (dact * tanh_part * gate_part * (1.0 - gate_part)).astype(jnp.bfloat16)
    dembed = prob[:, None] * pooled_gradient + jnp.dot(dtanh, att_tanh.T, preferred_element_type=jnp.float32)
    dembed = dembed + jnp.dot(dgate, att_gate.T, preferred_element_type=jnp.float32)
    dout = (dembed / POS).astype(jnp.bfloat16)
    spread = jnp.broadcast_to(dout[:, None, :], (rows, POS, CH)).reshape(rows * POS, CH)
    grad_w2 = jnp.dot(spread.T, hidden, preferred_element_type=jnp.float32)
    dhid = jnp.dot(spread, w_expand, preferred_element_type=jnp.float32)
    dhid = (dhid * (hidden > 0).astype(jnp.float32)).astype(jnp.bfloat16)
    grad_w1 = jnp.dot(flat.T, dhid, preferred_element_type=jnp.float32)
    return grad_w1, grad_w2, loss[None]
```

```python
import functools

import jax
import jax.numpy as jnp
from jax import lax
from jax.experimental import pallas as pl
from jax.experimental.pallas import tpu as pltpu
from jax.sharding import PartitionSpec as P

F32 = jnp.float32
BF16 = jnp.bfloat16
NY, NZ, NC = 4, 4, 2
ROWS = 32
PART = 4 * ROWS
NOTE = 16
VMEM_LIMIT = 48 * 1024 * 1024


def dot(a, b, dims):
    return lax.dot_general(a, b, (dims, ((), ())), preferred_element_type=F32)


def split3(x):
    high = x.astype(BF16)
    rest = x - high.astype(F32)
    mid = rest.astype(BF16)
    low = (rest - mid.astype(F32)).astype(BF16)
    return [high.astype(F32), mid.astype(F32), low.astype(F32)]


def note_rows(total, mean0, mean1):
    rows = split3(total) + split3(mean0) + split3(mean1)
    rows.append(jnp.zeros((NOTE - len(rows), rows[0].shape[1]), F32))
    return jnp.concatenate(rows, axis=0).astype(BF16)


def read_note(note):
    rows = note.astype(F32)
    return [rows[i : i + 1] + rows[i + 1 : i + 2] + rows[i + 2 : i + 3] for i in (0, 3, 6)]


def merge_notes(notes):
    total = sum(n[0] for n in notes)
    shares = [n[0] / total for n in notes]
    mean0 = sum(a * n[1] for a, n in zip(shares, notes))
    mean1 = sum(a * n[2] for a, n in zip(shares, notes))
    offsets = [(n[1] - n[2]) - (mean0 - mean1) for n in notes]
    return total, mean0, mean1, shares, offsets


def local_kernel(
    count_ref,
    tiles_ref,
    w_reduce_ref,
    w_expand_ref,
    att_tanh_ref,
    att_gate_ref,
    att_vector_ref,
    classifier_ref,
    keep_ref,
    send_ref,
):
    rows, width = tiles_ref.shape
    slots = rows // 16
    flat = tiles_ref[...]
    hidden = jnp.maximum(dot(flat, w_reduce_ref[...], ((1,), (0,))), 0.0).astype(BF16)
    tile_of = lax.broadcasted_iota(jnp.int32, (slots, rows), 0)
    row_of = lax.broadcasted_iota(jnp.int32, (slots, rows), 1)
    pool = (tile_of == lax.shift_right_logical(row_of, 4)).astype(F32).astype(BF16)
    tile_sum = dot(pool, flat, ((1,), (0,)))
    hidden_sum = dot(pool, hidden, ((1,), (0,)))
    sum_high = hidden_sum.astype(BF16)
    sum_low = (hidden_sum - sum_high.astype(F32)).astype(BF16)
    w_expand = w_expand_ref[...]
    expanded = dot(jnp.concatenate([sum_high, sum_low], axis=0), w_expand, ((1,), (1,)))
    embed = ((tile_sum + expanded[:slots] + expanded[slots:]) * (1.0 / 16.0)).astype(BF16)
    att_tanh, att_gate = att_tanh_ref[...], att_gate_ref[...]
    tanh_part = jnp.tanh(dot(embed, att_tanh, ((1,), (0,))))
    gate_part = jax.nn.sigmoid(dot(embed, att_gate, ((1,), (0,))))
    vector = att_vector_ref[...]
    score = jnp.sum(tanh_part * gate_part * vector, axis=1, keepdims=True)
    slot = lax.broadcasted_iota(jnp.int32, (slots, 1), 0)
    weight = jnp.where(slot < count_ref[0], jnp.exp(score), 0.0)
    total = jnp.sum(weight, axis=0, keepdims=True)
    share = weight / total
    embed_float = embed.astype(F32)
    class0, class1 = classifier_ref[0:1, :], classifier_ref[1:2, :]
    u0 = jnp.sum(embed_float * class0, axis=1, keepdims=True)
    u1 = jnp.sum(embed_float * class1, axis=1, keepdims=True)
    mean0 = jnp.sum(share * u0, axis=0, keepdims=True)
    mean1 = jnp.sum(share * u1, axis=0, keepdims=True)
    slope = share * ((u0 - u1) - (mean0 - mean1))
    e_tanh = (vector * gate_part * (1.0 - tanh_part * tanh_part)).astype(BF16)
    e_gate = (vector * tanh_part * gate_part * (1.0 - gate_part)).astype(BF16)
    path = dot(e_tanh, att_tanh, ((1,), (1,))) + dot(e_gate, att_gate, ((1,), (1,)))
    dy_a = ((share * (class0 - class1) + slope * path) * (1.0 / 16.0)).astype(BF16)
    dy_b = (share * path * (1.0 / 16.0)).astype(BF16)
    dy = jnp.concatenate([dy_a, dy_b], axis=0)
    back = dot(dy, w_expand, ((1,), (0,))).astype(BF16)
    back = jnp.concatenate([back[:slots], back[slots:]], axis=1)
    spread = dot(pool, back, ((0,), (0,)))
    hid = hidden.shape[1]
    mask = hidden.astype(F32) > 0
    dhid = jnp.concatenate(
        [jnp.where(mask, spread[:, :hid], 0.0), jnp.where(mask, spread[:, hid:], 0.0)], axis=1
    ).astype(BF16)
    grad_w1 = dot(flat, dhid, ((0,), (0,)))
    sums = jnp.concatenate([sum_high, sum_low], axis=0)
    w2_a = dot(jnp.concatenate([dy_a, dy_a], axis=0), sums, ((0,), (0,)))
    w2_b = dot(jnp.concatenate([dy_b, dy_b], axis=0), sums, ((0,), (0,)))
    first = lax.rem(lax.axis_index("tile"), NC) == 0
    parts = [grad_w1[:, :hid], w2_a, grad_w1[:, hid:], w2_b]
    note = note_rows(*[jnp.broadcast_to(v, (1, hid)) for v in (total, mean0, mean1)])
    for y in range(NY):
        for z in range(NZ):
            for i, part in enumerate(parts):
                at = (y * NZ + z) * NC * ROWS
                even = part[at : at + ROWS].astype(BF16)
                odd = part[at + ROWS : at + 2 * ROWS].astype(BF16)
                here = pl.ds(z * PART + i * ROWS, ROWS)
                keep_ref[y, here, :] = jnp.where(first, even, odd)
                send_ref[y, here, :] = jnp.where(first, odd, even)
        keep_ref[y, NZ * PART :, :] = note
        send_ref[y, NZ * PART :, :] = note


def merge(blocks, notes):
    total, mean0, mean1, shares, offsets = merge_notes(notes)
    sums = []
    for i in (0, 1):
        sums.append(sum(a * (b[i] + o * b[i + 2]) for a, o, b in zip(shares, offsets, blocks)))
    for i in (2, 3):
        sums.append(sum(a * b[i] for a, b in zip(shares, blocks)))
    return sums, note_rows(total, mean0, mean1)


def core_kernel(own_ref, other_ref, out_ref):
    tail = NZ * PART
    notes = [read_note(r[0, tail:, :]) for r in (own_ref, other_ref)]
    for y in range(NY):
        for z in range(NZ):
            blocks = [
                [r[y, z * PART + i * ROWS : z * PART + (i + 1) * ROWS, :].astype(F32) for i in range(4)]
                for r in (own_ref, other_ref)
            ]
            sums, note = merge(blocks, notes)
            for i in range(4):
                out_ref[y, pl.ds(z * PART + i * ROWS, ROWS), :] = sums[i].astype(BF16)
        out_ref[y, tail:, :] = note


def y_kernel(in_ref, out_ref):
    tail = NZ * PART
    notes = [read_note(in_ref[y, tail:, :]) for y in range(NY)]
    for z in range(NZ):
        blocks = [
            [in_ref[y, z * PART + i * ROWS : z * PART + (i + 1) * ROWS, :].astype(F32) for i in range(4)]
            for y in range(NY)
        ]
        sums, note = merge(blocks, notes)
        for i in range(4):
            out_ref[z, pl.ds(i * ROWS, ROWS), :] = sums[i].astype(BF16)
        out_ref[z, PART:, :] = note


def z_kernel(count, in_ref, target_ref, w1_ref, w2_ref, loss_ref):
    notes = [read_note(in_ref[z, PART:, :]) for z in range(NZ)]
    total, mean0, mean1, shares, offsets = merge_notes(notes)
    width = mean0.shape[1]
    target0 = jnp.full((1, width), target_ref[0], F32)
    target1 = jnp.full((1, width), target_ref[1], F32)
    target_sum = target0 + target1
    share0, share1 = target0 / target_sum, target1 / target_sum
    log_partition_sum = jnp.log(jnp.exp(mean0) + jnp.exp(mean1))
    loss = log_partition_sum - (mean0 * share0 + mean1 * share1)
    scale = count * (jnp.exp(mean0 - log_partition_sum) - share0)
    loss_ref[...] = loss[:, :128]
    for i, out_ref in enumerate((w1_ref, w2_ref)):
        result = 0.0
        for z in range(NZ):
            a = in_ref[z, i * ROWS : (i + 1) * ROWS, :].astype(F32)
            b = in_ref[z, (i + 2) * ROWS : (i + 3) * ROWS, :].astype(F32)
            result = result + shares[z] * (a + offsets[z] * b)
        out_ref[...] = scale * result


def vmem(count):
    return [pl.BlockSpec(memory_space=pltpu.VMEM)] * count


def call(kernel, out_shape, in_specs, args, name):
    many = isinstance(out_shape, (tuple, list))
    return pl.pallas_call(
        kernel,
        out_shape=out_shape,
        in_specs=in_specs,
        out_specs=tuple(vmem(len(out_shape))) if many else vmem(1)[0],
        compiler_params=pltpu.CompilerParams(vmem_limit_bytes=VMEM_LIMIT),
        name=name,
    )(*args)


def place(y, z, core):
    return (y * NZ + z) * NC + core


def body(
    tiles,
    w_reduce,
    w_expand,
    att_tanh,
    att_gate,
    att_vector,
    classifier,
    tile_counts,
    target_weights,
):
    slots, positions, width = tiles.shape
    hid = w_reduce.shape[1]
    smem = pl.BlockSpec(memory_space=pltpu.SMEM)
    chunk = jax.ShapeDtypeStruct((NY, NZ * PART + NOTE, hid), BF16)
    keep, send = call(
        local_kernel,
        (chunk, chunk),
        [smem] + vmem(7),
        (
            tile_counts,
            tiles.reshape(slots * positions, width),
            w_reduce,
            w_expand,
            att_tanh,
            att_gate,
            att_vector.reshape(1, hid),
            classifier.T,
        ),
        "local",
    )
    everyone = [(y, z, c) for y in range(NY) for z in range(NZ) for c in range(NC)]
    other = lax.ppermute(send, "tile", [(place(y, z, c), place(y, z, 1 - c)) for y, z, c in everyone])
    pair = call(core_kernel, chunk, vmem(2), (keep, other), "join_cores")
    along_y = [[place(y, z, c) for y in range(NY)] for z in range(NZ) for c in range(NC)]
    along_z = [[place(y, z, c) for z in range(NZ)] for y in range(NY) for c in range(NC)]
    pair = lax.all_to_all(pair, "tile", 0, 0, axis_index_groups=along_y, tiled=True)
    line = call(
        y_kernel, jax.ShapeDtypeStruct((NZ, PART + NOTE, hid), BF16), vmem(1), (pair,), "join_y"
    )
    line = lax.all_to_all(line, "tile", 0, 0, axis_index_groups=along_z, tiled=True)
    count = float(lax.axis_size("tile") * slots // 2)
    out = jax.ShapeDtypeStruct((ROWS, hid), F32)
    grad_w1, grad_w2, loss = call(
        functools.partial(z_kernel, count),
        (out, out, jax.ShapeDtypeStruct((1, 128), F32)),
        vmem(1) + [smem],
        (line, target_weights),
        "join_z",
    )
    return grad_w1, grad_w2, loss[0, :1]


def solution(mesh):
    placed = (
        P(("slide", "tile"), None, None),
        P(),
        P(),
        P(),
        P(),
        P(),
        P(),
        P(("slide", "tile")),
        P("slide"),
    )
    return jax.shard_map(
        body,
        mesh=mesh,
        in_specs=placed,
        out_specs=(P(("slide", "tile"), None), P(("slide", "tile"), None), P("slide")),
        check_vma=False,
    )
```

```python
import functools

import jax
import jax.numpy as jnp
from jax import lax
from jax.experimental import pallas as pl
from jax.experimental.pallas import tpu as pltpu
from jax.sharding import PartitionSpec as P

F32 = jnp.float32
BF16 = jnp.bfloat16
NY, NZ, NC = 4, 4, 2
ROWS = 32
PART = 8 * ROWS
HALF = PART // 2
TAIL = NZ * PART
NOTE = 16
VMEM_LIMIT = 48 * 1024 * 1024


def dot(a, b, dims):
    return lax.dot_general(a, b, (dims, ((), ())), preferred_element_type=F32)


def split3(x):
    high = x.astype(BF16)
    rest = x - high.astype(F32)
    mid = rest.astype(BF16)
    low = (rest - mid.astype(F32)).astype(BF16)
    return [high.astype(F32), mid.astype(F32), low.astype(F32)]


def note_rows(total, mean0, mean1):
    rows = split3(total) + split3(mean0) + split3(mean1)
    rows.append(jnp.zeros((NOTE - len(rows), rows[0].shape[1]), F32))
    return jnp.concatenate(rows, axis=0).astype(BF16)


def read_note(note):
    rows = note.astype(F32)
    return [rows[i : i + 1] + rows[i + 1 : i + 2] + rows[i + 2 : i + 3] for i in (0, 3, 6)]


def merge_notes(notes):
    total = sum(n[0] for n in notes)
    shares = [n[0] / total for n in notes]
    mean0 = sum(a * n[1] for a, n in zip(shares, notes))
    mean1 = sum(a * n[2] for a, n in zip(shares, notes))
    offsets = [(n[1] - n[2]) - (mean0 - mean1) for n in notes]
    return total, mean0, mean1, shares, offsets


def position_sum(x):
    return jnp.sum(x.reshape(x.shape[0] // 16, 16, x.shape[1]).astype(F32), axis=1)


def store_parts(part_a, part_b, which, keep_ref, send_ref):
    first = lax.rem(lax.axis_index("tile"), NC) == 0
    for y in range(NY):
        for z in range(NZ):
            at = (y * NZ + z) * NC * ROWS
            for i, part in enumerate((part_a, part_b)):
                for half in range(2):
                    cols = slice(half * 128, half * 128 + 128)
                    even = part[at : at + ROWS, cols].astype(BF16)
                    odd = part[at + ROWS : at + 2 * ROWS, cols].astype(BF16)
                    here = pl.ds(z * PART + (4 * i + 2 * which + half) * ROWS, ROWS)
                    keep_ref[y, here, :] = jnp.where(first, even, odd)
                    send_ref[y, here, :] = jnp.where(first, odd, even)


CHUNKS = 2


def local_kernel(
    count_ref,
    tiles_hbm,
    w_reduce_hbm,
    w_expand_hbm,
    att_tanh_hbm,
    att_gate_hbm,
    att_vector_hbm,
    classifier_hbm,
    keep_ref,
    send_ref,
    flat_ref,
    w_reduce_ref,
    w_expand_ref,
    att_tanh_ref,
    att_gate_ref,
    att_vector_ref,
    classifier_ref,
    hidden_ref,
    sem,
):
    rows, width = flat_ref.shape
    slots = rows // 16
    step = rows // CHUNKS
    copies = [pltpu.make_async_copy(w_reduce_hbm, w_reduce_ref, sem.at[CHUNKS])]
    for i in range(CHUNKS):
        part = pl.ds(i * step, step)
        copies.append(pltpu.make_async_copy(tiles_hbm.at[part], flat_ref.at[part], sem.at[i]))
    copies.append(pltpu.make_async_copy(w_expand_hbm, w_expand_ref, sem.at[CHUNKS + 1]))
    copies.append(pltpu.make_async_copy(att_tanh_hbm, att_tanh_ref, sem.at[CHUNKS + 2]))
    copies.append(pltpu.make_async_copy(att_gate_hbm, att_gate_ref, sem.at[CHUNKS + 3]))
    copies.append(pltpu.make_async_copy(att_vector_hbm, att_vector_ref, sem.at[CHUNKS + 4]))
    copies.append(pltpu.make_async_copy(classifier_hbm, classifier_ref, sem.at[CHUNKS + 5]))
    for copy in copies:
        copy.start()
    copies[0].wait()
    w_reduce = w_reduce_ref[...]
    tile_sums, hidden_sums = [], []
    for i in range(CHUNKS):
        copies[1 + i].wait()
        part = pl.ds(i * step, step)
        flat = flat_ref[part, :]
        hidden = jnp.maximum(dot(flat, w_reduce, ((1,), (0,))), 0.0).astype(BF16)
        hidden_ref[part, :] = hidden
        tile_sums.append(position_sum(flat))
        hidden_sums.append(position_sum(hidden))
    tile_sum = jnp.concatenate(tile_sums, axis=0)
    hidden_sum = jnp.concatenate(hidden_sums, axis=0)
    sum_high = hidden_sum.astype(BF16)
    sum_low = (hidden_sum - sum_high.astype(F32)).astype(BF16)
    copies[CHUNKS + 1].wait()
    w_expand = w_expand_ref[...]
    sums = jnp.concatenate([sum_high, sum_low], axis=0)
    expanded = dot(sums, w_expand, ((1,), (1,)))
    embed = ((tile_sum + expanded[:slots] + expanded[slots:]) * (1.0 / 16.0)).astype(BF16)
    for copy in copies[CHUNKS + 2 :]:
        copy.wait()
    att_tanh, att_gate = att_tanh_ref[...], att_gate_ref[...]
    tanh_part = jnp.tanh(dot(embed, att_tanh, ((1,), (0,))))
    gate_part = jax.nn.sigmoid(dot(embed, att_gate, ((1,), (0,))))
    vector = att_vector_ref[...]
    score = jnp.sum(tanh_part * gate_part * vector, axis=1, keepdims=True)
    slot = lax.broadcasted_iota(jnp.int32, (slots, 1), 0)
    weight = jnp.where(slot < count_ref[0], jnp.exp(score), 0.0)
    total = jnp.sum(weight, axis=0, keepdims=True)
    share = weight / total
    embed_float = embed.astype(F32)
    class0, class1 = classifier_ref[0:1, :], classifier_ref[1:2, :]
    u0 = jnp.sum(embed_float * class0, axis=1, keepdims=True)
    u1 = jnp.sum(embed_float * class1, axis=1, keepdims=True)
    mean0 = jnp.sum(share * u0, axis=0, keepdims=True)
    mean1 = jnp.sum(share * u1, axis=0, keepdims=True)
    slope = share * ((u0 - u1) - (mean0 - mean1))
    e_tanh = (vector * gate_part * (1.0 - tanh_part * tanh_part)).astype(BF16)
    e_gate = (vector * tanh_part * gate_part * (1.0 - gate_part)).astype(BF16)
    path = dot(e_tanh, att_tanh, ((1,), (1,))) + dot(e_gate, att_gate, ((1,), (1,)))
    dy_a = ((share * (class0 - class1) + slope * path) * (1.0 / 16.0)).astype(BF16)
    dy_b = (share * path * (1.0 / 16.0)).astype(BF16)
    w2_a = dot(jnp.concatenate([dy_a, dy_a], axis=0), sums, ((0,), (0,)))
    w2_b = dot(jnp.concatenate([dy_b, dy_b], axis=0), sums, ((0,), (0,)))
    store_parts(w2_a, w2_b, 1, keep_ref, send_ref)
    note = note_rows(*[jnp.broadcast_to(v, (1, 128)) for v in (total, mean0, mean1)])
    for y in range(NY):
        keep_ref[y, TAIL:, :] = note
        send_ref[y, TAIL:, :] = note
    back = dot(jnp.concatenate([dy_a, dy_b], axis=0), w_expand, ((1,), (0,))).astype(BF16)
    back = jnp.concatenate([back[:slots], back[slots:]], axis=1)
    spread = jnp.broadcast_to(back.astype(F32)[:, None, :], (slots, 16, back.shape[1]))
    spread = spread.reshape(rows, back.shape[1])
    mask = hidden_ref[...].astype(F32) > 0
    hid = mask.shape[1]
    dhid = jnp.concatenate(
        [jnp.where(mask, spread[:, :hid], 0.0), jnp.where(mask, spread[:, hid:], 0.0)], axis=1
    ).astype(BF16)
    grad_w1 = dot(flat_ref[...], dhid, ((0,), (0,)))
    store_parts(grad_w1[:, :hid], grad_w1[:, hid:], 0, keep_ref, send_ref)


def merge(blocks, shares, offsets):
    a = b = 0.0
    for share, offset, block in zip(shares, offsets, blocks):
        block_b = block[HALF:].astype(F32)
        a = a + share * (block[:HALF].astype(F32) + offset * block_b)
        b = b + share * block_b
    return a.astype(BF16), b.astype(BF16)


def core_kernel(own_ref, other_ref, *out_refs):
    notes = [read_note(r[0, TAIL:, :]) for r in (own_ref, other_ref)]
    total, mean0, mean1, shares, offsets = merge_notes(notes)
    note = note_rows(total, mean0, mean1)
    here = lax.div(lax.axis_index("tile"), NZ * NC)
    for away, out_ref in enumerate(out_refs):
        y = lax.rem(here + away, NY)
        for z in range(NZ):
            part = slice(z * PART, (z + 1) * PART)
            a, b = merge([r[y, part, :] for r in (own_ref, other_ref)], shares, offsets)
            out_ref[z * PART : z * PART + HALF, :] = a
            out_ref[z * PART + HALF : (z + 1) * PART, :] = b
        out_ref[TAIL:, :] = note


def y_kernel(in0, in1, in2, in3, *out_refs):
    in_refs = (in0, in1, in2, in3)
    notes = [read_note(r[TAIL:, :]) for r in in_refs]
    total, mean0, mean1, shares, offsets = merge_notes(notes)
    note = note_rows(total, mean0, mean1)
    here = lax.rem(lax.div(lax.axis_index("tile"), NC), NZ)
    for away, out_ref in enumerate(out_refs):
        z = lax.rem(here + away, NZ)
        part = pl.ds(pl.multiple_of(z * PART, PART), PART)
        a, b = merge([r[part, :] for r in in_refs], shares, offsets)
        out_ref[:HALF, :] = a
        out_ref[HALF:PART, :] = b
        out_ref[PART:, :] = note


def z_kernel(count, in0, in1, in2, in3, target_ref, w1_ref, w2_ref, loss_ref):
    in_refs = (in0, in1, in2, in3)
    notes = [read_note(r[PART:, :]) for r in in_refs]
    total, mean0, mean1, shares, offsets = merge_notes(notes)
    width = mean0.shape[1]
    target0 = jnp.full((1, width), target_ref[0], F32)
    target1 = jnp.full((1, width), target_ref[1], F32)
    target_sum = target0 + target1
    share0, share1 = target0 / target_sum, target1 / target_sum
    log_partition_sum = jnp.log(jnp.exp(mean0) + jnp.exp(mean1))
    loss_ref[...] = log_partition_sum - (mean0 * share0 + mean1 * share1)
    scale = count * (jnp.exp(mean0 - log_partition_sum) - share0)
    for i, out_ref in enumerate((w1_ref, w2_ref)):
        result = 0.0
        for share, offset, r in zip(shares, offsets, in_refs):
            a = r[2 * i * ROWS : 2 * (i + 1) * ROWS, :].astype(F32)
            b = r[HALF + 2 * i * ROWS : HALF + 2 * (i + 1) * ROWS, :].astype(F32)
            result = result + share * (a + offset * b)
        result = scale * result
        out_ref[:, :width] = result[:ROWS]
        out_ref[:, width:] = result[ROWS:]


def vmem(count):
    return [pl.BlockSpec(memory_space=pltpu.VMEM)] * count


def call(kernel, out_shape, in_specs, args, name, scratch=()):
    many = isinstance(out_shape, (tuple, list))
    return pl.pallas_call(
        kernel,
        out_shape=out_shape,
        in_specs=in_specs,
        out_specs=tuple(vmem(len(out_shape))) if many else vmem(1)[0],
        scratch_shapes=list(scratch),
        compiler_params=pltpu.CompilerParams(vmem_limit_bytes=VMEM_LIMIT),
        name=name,
    )(*args)


def place(y, z, core):
    return (y * NZ + z) * NC + core


def body(
    tiles,
    w_reduce,
    w_expand,
    att_tanh,
    att_gate,
    att_vector,
    classifier,
    tile_counts,
    target_weights,
):
    slots, positions, width = tiles.shape
    rows = slots * positions
    hid = w_reduce.shape[1]
    smem = pl.BlockSpec(memory_space=pltpu.SMEM)
    hbm = pl.BlockSpec(memory_space=pltpu.HBM)
    held = [
        pltpu.with_memory_space_constraint(x, pltpu.HBM)
        for x in (
            tiles.reshape(rows, width),
            w_reduce,
            w_expand,
            att_tanh,
            att_gate,
            att_vector.reshape(1, hid),
            classifier.T,
        )
    ]
    chunk = jax.ShapeDtypeStruct((NY, TAIL + NOTE, 128), BF16)
    keep, send = call(
        local_kernel,
        (chunk, chunk),
        [smem] + [hbm] * 7,
        (tile_counts, *held),
        "local",
        [pltpu.VMEM((rows, width), BF16)]
        + [pltpu.VMEM((width, hid), BF16)] * 4
        + [pltpu.VMEM((1, hid), F32), pltpu.VMEM((2, width), F32)]
        + [pltpu.VMEM((rows, hid), BF16), pltpu.SemaphoreType.DMA((CHUNKS + 6,))],
    )
    everyone = [(y, z, c) for y in range(NY) for z in range(NZ) for c in range(NC)]

    def move(x, dy, dz, dc):
        pairs = [
            (place(y, z, c), place((y + dy) % NY, (z + dz) % NZ, (c + dc) % NC)) for y, z, c in everyone
        ]
        return lax.ppermute(x, "tile", pairs)

    other = move(send, 0, 0, 1)
    piece = jax.ShapeDtypeStruct((TAIL + NOTE, 128), BF16)
    pieces = call(core_kernel, (piece,) * NY, vmem(2), (keep, other), "join_cores")
    across = [move(pieces[2], 2, 0, 0), move(pieces[1], 1, 0, 0), move(pieces[3], 3, 0, 0)]
    piece = jax.ShapeDtypeStruct((PART + NOTE, 128), BF16)
    pieces = call(y_kernel, (piece,) * NZ, vmem(NY), (pieces[0], *across), "join_y")
    across = [move(pieces[2], 0, 2, 0), move(pieces[1], 0, 1, 0), move(pieces[3], 0, 3, 0)]
    count = float(lax.axis_size("tile") * slots // 2)
    out = jax.ShapeDtypeStruct((ROWS, hid), F32)
    grad_w1, grad_w2, loss = call(
        functools.partial(z_kernel, count),
        (out, out, jax.ShapeDtypeStruct((1, 128), F32)),
        vmem(NZ) + [smem],
        (pieces[0], *across, target_weights),
        "join_z",
    )
    return grad_w1, grad_w2, loss[0, :1]


def solution(mesh):
    placed = (
        P(("slide", "tile"), None, None),
        P(),
        P(),
        P(),
        P(),
        P(),
        P(),
        P(("slide", "tile")),
        P("slide"),
    )
    return jax.shard_map(
        body,
        mesh=mesh,
        in_specs=placed,
        out_specs=(P(("slide", "tile"), None), P(("slide", "tile"), None), P("slide")),
        check_vma=False,
    )
```

```python
import functools

import jax
import jax.numpy as jnp
from jax import lax
from jax.experimental import pallas as pl
from jax.experimental.pallas import tpu as pltpu
from jax.sharding import PartitionSpec as P

F32 = jnp.float32
BF16 = jnp.bfloat16
NY, NZ, NC = 4, 4, 2
ROWS = 32
PART = 8 * ROWS
HALF = PART // 2
TAIL = NZ * PART
NOTE = 16
VMEM_LIMIT = 48 * 1024 * 1024


def dot(a, b, dims):
    return lax.dot_general(a, b, (dims, ((), ())), preferred_element_type=F32)


def split3(x):
    high = x.astype(BF16)
    rest = x - high.astype(F32)
    mid = rest.astype(BF16)
    low = (rest - mid.astype(F32)).astype(BF16)
    return [high.astype(F32), mid.astype(F32), low.astype(F32)]


def note_rows(total, mean0, mean1):
    rows = split3(total) + split3(mean0) + split3(mean1)
    rows.append(jnp.zeros((NOTE - len(rows), rows[0].shape[1]), F32))
    return jnp.concatenate(rows, axis=0).astype(BF16)


def read_note(note):
    rows = note.astype(F32)
    return [rows[i : i + 1] + rows[i + 1 : i + 2] + rows[i + 2 : i + 3] for i in (0, 3, 6)]


def merge_notes(notes):
    total = sum(n[0] for n in notes)
    shares = [n[0] / total for n in notes]
    mean0 = sum(a * n[1] for a, n in zip(shares, notes))
    mean1 = sum(a * n[2] for a, n in zip(shares, notes))
    offsets = [(n[1] - n[2]) - (mean0 - mean1) for n in notes]
    return total, mean0, mean1, shares, offsets


def position_sum(x):
    return jnp.sum(x.reshape(x.shape[0] // 16, 16, x.shape[1]).astype(F32), axis=1)


def store_parts(part_a, part_b, which, keep_ref, send_ref):
    first = lax.rem(lax.axis_index("tile"), NC) == 0
    for y in range(NY):
        for z in range(NZ):
            at = (y * NZ + z) * NC * ROWS
            for i, part in enumerate((part_a, part_b)):
                for half in range(2):
                    cols = slice(half * 128, half * 128 + 128)
                    even = part[at : at + ROWS, cols].astype(BF16)
                    odd = part[at + ROWS : at + 2 * ROWS, cols].astype(BF16)
                    here = pl.ds(z * PART + (4 * i + 2 * which + half) * ROWS, ROWS)
                    keep_ref[y, here, :] = jnp.where(first, even, odd)
                    send_ref[y, here, :] = jnp.where(first, odd, even)


CHUNKS = 2


def local_kernel(
    count_ref,
    tiles_hbm,
    w_reduce_hbm,
    w_expand_hbm,
    att_tanh_hbm,
    att_gate_hbm,
    att_vector_hbm,
    classifier_hbm,
    keep_ref,
    send_ref,
    flat_ref,
    w_reduce_ref,
    w_expand_ref,
    att_tanh_ref,
    att_gate_ref,
    att_vector_ref,
    classifier_ref,
    hidden_ref,
    sem,
):
    rows, width = flat_ref.shape
    slots = rows // 16
    step = rows // CHUNKS
    copies = [pltpu.make_async_copy(w_reduce_hbm, w_reduce_ref, sem.at[CHUNKS])]
    for i in range(CHUNKS):
        part = pl.ds(i * step, step)
        copies.append(pltpu.make_async_copy(tiles_hbm.at[part], flat_ref.at[part], sem.at[i]))
    copies.append(pltpu.make_async_copy(w_expand_hbm, w_expand_ref, sem.at[CHUNKS + 1]))
    copies.append(pltpu.make_async_copy(att_tanh_hbm, att_tanh_ref, sem.at[CHUNKS + 2]))
    copies.append(pltpu.make_async_copy(att_gate_hbm, att_gate_ref, sem.at[CHUNKS + 3]))
    copies.append(pltpu.make_async_copy(att_vector_hbm, att_vector_ref, sem.at[CHUNKS + 4]))
    copies.append(pltpu.make_async_copy(classifier_hbm, classifier_ref, sem.at[CHUNKS + 5]))
    for copy in copies:
        copy.start()
    copies[0].wait()
    w_reduce = w_reduce_ref[...]
    tile_sums, hidden_sums = [], []
    for i in range(CHUNKS):
        copies[1 + i].wait()
        part = pl.ds(i * step, step)
        flat = flat_ref[part, :]
        hidden = jnp.maximum(dot(flat, w_reduce, ((1,), (0,))), 0.0).astype(BF16)
        hidden_ref[part, :] = hidden
        tile_sums.append(position_sum(flat))
        hidden_sums.append(position_sum(hidden))
    tile_sum = jnp.concatenate(tile_sums, axis=0)
    hidden_sum = jnp.concatenate(hidden_sums, axis=0)
    sum_high = hidden_sum.astype(BF16)
    sum_low = (hidden_sum - sum_high.astype(F32)).astype(BF16)
    copies[CHUNKS + 1].wait()
    w_expand = w_expand_ref[...]
    sums = jnp.concatenate([sum_high, sum_low], axis=0)
    expanded = dot(sums, w_expand, ((1,), (1,)))
    embed = ((tile_sum + expanded[:slots] + expanded[slots:]) * (1.0 / 16.0)).astype(BF16)
    for copy in copies[CHUNKS + 2 :]:
        copy.wait()
    att_tanh, att_gate = att_tanh_ref[...], att_gate_ref[...]
    tanh_part = jnp.tanh(dot(embed, att_tanh, ((1,), (0,))))
    gate_part = jax.nn.sigmoid(dot(embed, att_gate, ((1,), (0,))))
    vector = att_vector_ref[...]
    score = jnp.sum(tanh_part * gate_part * vector, axis=1, keepdims=True)
    slot = lax.broadcasted_iota(jnp.int32, (slots, 1), 0)
    weight = jnp.where(slot < count_ref[0], jnp.exp(score), 0.0)
    total = jnp.sum(weight, axis=0, keepdims=True)
    share = weight / total
    embed_float = embed.astype(F32)
    class0, class1 = classifier_ref[0:1, :], classifier_ref[1:2, :]
    u0 = jnp.sum(embed_float * class0, axis=1, keepdims=True)
    u1 = jnp.sum(embed_float * class1, axis=1, keepdims=True)
    mean0 = jnp.sum(share * u0, axis=0, keepdims=True)
    mean1 = jnp.sum(share * u1, axis=0, keepdims=True)
    slope = share * ((u0 - u1) - (mean0 - mean1))
    e_tanh = (vector * gate_part * (1.0 - tanh_part * tanh_part)).astype(BF16)
    e_gate = (vector * tanh_part * gate_part * (1.0 - gate_part)).astype(BF16)
    path = dot(e_tanh, att_tanh, ((1,), (1,))) + dot(e_gate, att_gate, ((1,), (1,)))
    dy_a = ((share * (class0 - class1) + slope * path) * (1.0 / 16.0)).astype(BF16)
    dy_b = (share * path * (1.0 / 16.0)).astype(BF16)
    w2_a = dot(jnp.concatenate([dy_a, dy_a], axis=0), sums, ((0,), (0,)))
    w2_b = dot(jnp.concatenate([dy_b, dy_b], axis=0), sums, ((0,), (0,)))
    store_parts(w2_a, w2_b, 1, keep_ref, send_ref)
    note = note_rows(*[jnp.broadcast_to(v, (1, 128)) for v in (total, mean0, mean1)])
    for y in range(NY):
        keep_ref[y, TAIL:, :] = note
        send_ref[y, TAIL:, :] = note
    back = dot(jnp.concatenate([dy_a, dy_b], axis=0), w_expand, ((1,), (0,))).astype(BF16)
    back = jnp.concatenate([back[:slots], back[slots:]], axis=1)
    spread = jnp.broadcast_to(back.astype(F32)[:, None, :], (slots, 16, back.shape[1]))
    spread = spread.reshape(rows, back.shape[1])
    mask = hidden_ref[...].astype(F32) > 0
    hid = mask.shape[1]
    dhid = jnp.concatenate(
        [jnp.where(mask, spread[:, :hid], 0.0), jnp.where(mask, spread[:, hid:], 0.0)], axis=1
    ).astype(BF16)
    grad_w1 = dot(flat_ref[...], dhid, ((0,), (0,)))
    store_parts(grad_w1[:, :hid], grad_w1[:, hid:], 0, keep_ref, send_ref)


def merge(blocks, shares, offsets):
    a = b = 0.0
    for share, offset, block in zip(shares, offsets, blocks):
        block_b = block[HALF:].astype(F32)
        a = a + share * (block[:HALF].astype(F32) + offset * block_b)
        b = b + share * block_b
    return a.astype(BF16), b.astype(BF16)


def core_kernel(own_ref, other_ref, *out_refs):
    notes = [read_note(r[0, TAIL:, :]) for r in (own_ref, other_ref)]
    total, mean0, mean1, shares, offsets = merge_notes(notes)
    note = note_rows(total, mean0, mean1)
    here = lax.div(lax.axis_index("tile"), NZ * NC)
    for away, out_ref in enumerate(out_refs):
        y = lax.rem(here + away, NY)
        for z in range(NZ):
            part = slice(z * PART, (z + 1) * PART)
            a, b = merge([r[y, part, :] for r in (own_ref, other_ref)], shares, offsets)
            out_ref[z * PART : z * PART + HALF, :] = a
            out_ref[z * PART + HALF : (z + 1) * PART, :] = b
        out_ref[TAIL:, :] = note


def y_kernel(in0, in1, in2, in3, *out_refs):
    in_refs = (in0, in1, in2, in3)
    notes = [read_note(r[TAIL:, :]) for r in in_refs]
    total, mean0, mean1, shares, offsets = merge_notes(notes)
    note = note_rows(total, mean0, mean1)
    here = lax.rem(lax.div(lax.axis_index("tile"), NC), NZ)
    for away, out_ref in enumerate(out_refs):
        z = lax.bitwise_xor(here, away)
        part = pl.ds(pl.multiple_of(z * PART, PART), PART)
        a, b = merge([r[part, :] for r in in_refs], shares, offsets)
        out_ref[:HALF, :] = a
        out_ref[HALF:PART, :] = b
        out_ref[PART:, :] = note


def z_kernel(count, in0, in1, in2, in3, target_ref, w1_ref, w2_ref, loss_ref):
    in_refs = (in0, in1, in2, in3)
    notes = [read_note(r[PART:, :]) for r in in_refs]
    total, mean0, mean1, shares, offsets = merge_notes(notes)
    width = mean0.shape[1]
    target0 = jnp.full((1, width), target_ref[0], F32)
    target1 = jnp.full((1, width), target_ref[1], F32)
    target_sum = target0 + target1
    share0, share1 = target0 / target_sum, target1 / target_sum
    log_partition_sum = jnp.log(jnp.exp(mean0) + jnp.exp(mean1))
    loss_ref[...] = log_partition_sum - (mean0 * share0 + mean1 * share1)
    scale = count * (jnp.exp(mean0 - log_partition_sum) - share0)
    for i, out_ref in enumerate((w1_ref, w2_ref)):
        result = 0.0
        for share, offset, r in zip(shares, offsets, in_refs):
            a = r[2 * i * ROWS : 2 * (i + 1) * ROWS, :].astype(F32)
            b = r[HALF + 2 * i * ROWS : HALF + 2 * (i + 1) * ROWS, :].astype(F32)
            result = result + share * (a + offset * b)
        result = scale * result
        out_ref[:, :width] = result[:ROWS]
        out_ref[:, width:] = result[ROWS:]


def vmem(count):
    return [pl.BlockSpec(memory_space=pltpu.VMEM)] * count


def call(kernel, out_shape, in_specs, args, name, scratch=()):
    many = isinstance(out_shape, (tuple, list))
    return pl.pallas_call(
        kernel,
        out_shape=out_shape,
        in_specs=in_specs,
        out_specs=tuple(vmem(len(out_shape))) if many else vmem(1)[0],
        scratch_shapes=list(scratch),
        compiler_params=pltpu.CompilerParams(vmem_limit_bytes=VMEM_LIMIT),
        name=name,
    )(*args)


def place(y, z, core):
    return (y * NZ + z) * NC + core


def body(
    tiles,
    w_reduce,
    w_expand,
    att_tanh,
    att_gate,
    att_vector,
    classifier,
    tile_counts,
    target_weights,
):
    slots, positions, width = tiles.shape
    rows = slots * positions
    hid = w_reduce.shape[1]
    smem = pl.BlockSpec(memory_space=pltpu.SMEM)
    hbm = pl.BlockSpec(memory_space=pltpu.HBM)
    held = [
        pltpu.with_memory_space_constraint(x, pltpu.HBM)
        for x in (
            tiles.reshape(rows, width),
            w_reduce,
            w_expand,
            att_tanh,
            att_gate,
            att_vector.reshape(1, hid),
            classifier.T,
        )
    ]
    chunk = jax.ShapeDtypeStruct((NY, TAIL + NOTE, 128), BF16)
    keep, send = call(
        local_kernel,
        (chunk, chunk),
        [smem] + [hbm] * 7,
        (tile_counts, *held),
        "local",
        [pltpu.VMEM((rows, width), BF16)]
        + [pltpu.VMEM((width, hid), BF16)] * 4
        + [pltpu.VMEM((1, hid), F32), pltpu.VMEM((2, width), F32)]
        + [pltpu.VMEM((rows, hid), BF16), pltpu.SemaphoreType.DMA((CHUNKS + 6,))],
    )
    everyone = [(y, z, c) for y in range(NY) for z in range(NZ) for c in range(NC)]

    def move(x, dy, dz, dc):
        pairs = [
            (place(y, z, c), place((y + dy) % NY, (z + dz) % NZ, (c + dc) % NC)) for y, z, c in everyone
        ]
        return lax.ppermute(x, "tile", pairs)

    def swap(x, dy, dz):
        return lax.ppermute(x, "tile", [(place(y, z, c), place(y ^ dy, z ^ dz, c)) for y, z, c in everyone])

    other = move(send, 0, 0, 1)
    piece = jax.ShapeDtypeStruct((TAIL + NOTE, 128), BF16)
    pieces = call(core_kernel, (piece,) * NY, vmem(2), (keep, other), "join_cores")
    across = [move(pieces[2], 2, 0, 0), move(pieces[1], 1, 0, 0), move(pieces[3], 3, 0, 0)]
    piece = jax.ShapeDtypeStruct((PART + NOTE, 128), BF16)
    pieces = call(y_kernel, (piece,) * NZ, vmem(NY), (pieces[0], *across), "join_y")
    across = [swap(pieces[2], 0, 2), swap(pieces[3], 0, 3), swap(pieces[1], 0, 1)]
    count = float(lax.axis_size("tile") * slots // 2)
    out = jax.ShapeDtypeStruct((ROWS, hid), F32)
    grad_w1, grad_w2, loss = call(
        functools.partial(z_kernel, count),
        (out, out, jax.ShapeDtypeStruct((1, 128), F32)),
        vmem(NZ) + [smem],
        (pieces[0], *across, target_weights),
        "join_z",
    )
    return grad_w1, grad_w2, loss[0, :1]


def solution(mesh):
    placed = (
        P(("slide", "tile"), None, None),
        P(),
        P(),
        P(),
        P(),
        P(),
        P(),
        P(("slide", "tile")),
        P("slide"),
    )
    return jax.shard_map(
        body,
        mesh=mesh,
        in_specs=placed,
        out_specs=(P(("slide", "tile"), None), P(("slide", "tile"), None), P("slide")),
        check_vma=False,
    )
```

```python
import functools

import jax
import jax.numpy as jnp
from jax import lax
from jax.experimental import pallas as pl
from jax.experimental.pallas import tpu as pltpu
from jax.sharding import PartitionSpec as P

F32 = jnp.float32
BF16 = jnp.bfloat16
NY, NZ, NC = 4, 4, 2
ROWS = 32
PART = 8 * ROWS
HALF = PART // 2
W1_PART = 4 * ROWS
W1_ROWS = NZ * W1_PART
PATH_ROWS = NZ * ROWS
SLOTS = 64
CORE_PATH = NY * W1_ROWS
CORE_SUMS = CORE_PATH + NY * PATH_ROWS
CORE_NOTE = CORE_SUMS + 2 * SLOTS
Y_SUMS = W1_ROWS + PATH_ROWS
Y_NOTE = Y_SUMS + 4 * SLOTS
NOTE = 16
VMEM_LIMIT = 48 * 1024 * 1024


def dot(a, b, dims):
    return lax.dot_general(a, b, (dims, ((), ())), preferred_element_type=F32)


def split3(x):
    high = x.astype(BF16)
    rest = x - high.astype(F32)
    mid = rest.astype(BF16)
    low = (rest - mid.astype(F32)).astype(BF16)
    return [high.astype(F32), mid.astype(F32), low.astype(F32)]


def note_rows(*values):
    rows = [part for value in values for part in split3(value)]
    if len(rows) < NOTE:
        rows.append(jnp.zeros((NOTE - len(rows), rows[0].shape[1]), F32))
    return jnp.concatenate(rows, axis=0).astype(BF16)


def read_note(note, count):
    rows = note.astype(F32)
    return [
        rows[i : i + 1] + rows[i + 1 : i + 2] + rows[i + 2 : i + 3] for i in range(0, 3 * count, 3)
    ]


def merge_notes(notes):
    total = sum(n[0] for n in notes)
    shares = [n[0] / total for n in notes]
    mean0 = sum(a * n[1] for a, n in zip(shares, notes))
    mean1 = sum(a * n[2] for a, n in zip(shares, notes))
    offsets = [(n[1] - n[2]) - (mean0 - mean1) for n in notes]
    return total, mean0, mean1, shares, offsets


def position_sum(x):
    return jnp.sum(x.reshape(x.shape[0] // 16, 16, x.shape[1]).astype(F32), axis=1)


def store_w1(part_a, part_b, keep_ref, send_ref):
    first = lax.rem(lax.axis_index("tile"), NC) == 0
    for y in range(NY):
        for z in range(NZ):
            at = (y * NZ + z) * NC * ROWS
            for i, part in enumerate((part_a, part_b)):
                for half in range(2):
                    cols = slice(half * 128, half * 128 + 128)
                    even = part[at : at + ROWS, cols].astype(BF16)
                    odd = part[at + ROWS : at + 2 * ROWS, cols].astype(BF16)
                    here = pl.ds(y * W1_ROWS + z * W1_PART + (2 * i + half) * ROWS, ROWS)
                    keep_ref[here, :] = jnp.where(first, even, odd)
                    send_ref[here, :] = jnp.where(first, odd, even)


def store_path(path, keep_ref, send_ref):
    first = lax.rem(lax.axis_index("tile"), NC) == 0
    for k in range(NY * NZ):
        at = k * NC * ROWS
        even, odd = path[at : at + ROWS], path[at + ROWS : at + 2 * ROWS]
        here = pl.ds(CORE_PATH + k * ROWS, ROWS)
        keep_ref[here, :] = jnp.where(first, even[:, :128], odd[:, :128]).astype(BF16)
        send_ref[here, :] = jnp.where(first, odd[:, 128:], even[:, 128:]).astype(BF16)


def as_row(column, shift):
    slot = lax.broadcasted_iota(jnp.int32, (column.shape[0], 128), 0)
    lane = lax.broadcasted_iota(jnp.int32, (column.shape[0], 128), 1)
    return jnp.sum(jnp.where(slot + shift == lane, column, 0.0), axis=0, keepdims=True)


CHUNKS = 2


def local_kernel(
    count_ref,
    tiles_hbm,
    w_reduce_hbm,
    w_expand_hbm,
    att_tanh_hbm,
    att_gate_hbm,
    att_vector_hbm,
    classifier_hbm,
    keep_ref,
    send_ref,
    flat_ref,
    w_reduce_ref,
    w_expand_ref,
    att_tanh_ref,
    att_gate_ref,
    att_vector_ref,
    classifier_ref,
    hidden_ref,
    sem,
):
    rows, width = flat_ref.shape
    slots = rows // 16
    step = rows // CHUNKS
    copies = [pltpu.make_async_copy(w_reduce_hbm, w_reduce_ref, sem.at[CHUNKS])]
    for i in range(CHUNKS):
        part = pl.ds(i * step, step)
        copies.append(pltpu.make_async_copy(tiles_hbm.at[part], flat_ref.at[part], sem.at[i]))
    copies.append(pltpu.make_async_copy(w_expand_hbm, w_expand_ref, sem.at[CHUNKS + 1]))
    copies.append(pltpu.make_async_copy(att_tanh_hbm, att_tanh_ref, sem.at[CHUNKS + 2]))
    copies.append(pltpu.make_async_copy(att_gate_hbm, att_gate_ref, sem.at[CHUNKS + 3]))
    copies.append(pltpu.make_async_copy(att_vector_hbm, att_vector_ref, sem.at[CHUNKS + 4]))
    copies.append(pltpu.make_async_copy(classifier_hbm, classifier_ref, sem.at[CHUNKS + 5]))
    for copy in copies:
        copy.start()
    copies[0].wait()
    w_reduce = w_reduce_ref[...]
    tile_sums, hidden_sums = [], []
    for i in range(CHUNKS):
        copies[1 + i].wait()
        part = pl.ds(i * step, step)
        flat = flat_ref[part, :]
        hidden = jnp.maximum(dot(flat, w_reduce, ((1,), (0,))), 0.0).astype(BF16)
        hidden_ref[part, :] = hidden
        tile_sums.append(position_sum(flat))
        hidden_sums.append(position_sum(hidden))
    tile_sum = jnp.concatenate(tile_sums, axis=0)
    hidden_sum = jnp.concatenate(hidden_sums, axis=0)
    sum_high = hidden_sum.astype(BF16)
    sum_low = (hidden_sum - sum_high.astype(F32)).astype(BF16)
    copies[CHUNKS + 1].wait()
    w_expand = w_expand_ref[...]
    sums = jnp.concatenate([sum_high, sum_low], axis=0)
    expanded = dot(sums, w_expand, ((1,), (1,)))
    embed = ((tile_sum + expanded[:slots] + expanded[slots:]) * (1.0 / 16.0)).astype(BF16)
    for copy in copies[CHUNKS + 2 :]:
        copy.wait()
    att_tanh, att_gate = att_tanh_ref[...], att_gate_ref[...]
    tanh_part = jnp.tanh(dot(embed, att_tanh, ((1,), (0,))))
    gate_part = jax.nn.sigmoid(dot(embed, att_gate, ((1,), (0,))))
    vector = att_vector_ref[...]
    score = jnp.sum(tanh_part * gate_part * vector, axis=1, keepdims=True)
    slot = lax.broadcasted_iota(jnp.int32, (slots, 1), 0)
    weight = jnp.where(slot < count_ref[0], jnp.exp(score), 0.0)
    total = jnp.sum(weight, axis=0, keepdims=True)
    share = weight / total
    embed_float = embed.astype(F32)
    class0, class1 = classifier_ref[0:1, :], classifier_ref[1:2, :]
    u0 = jnp.sum(embed_float * class0, axis=1, keepdims=True)
    u1 = jnp.sum(embed_float * class1, axis=1, keepdims=True)
    mean0 = jnp.sum(share * u0, axis=0, keepdims=True)
    mean1 = jnp.sum(share * u1, axis=0, keepdims=True)
    slope = share * ((u0 - u1) - (mean0 - mean1))
    e_tanh = (vector * gate_part * (1.0 - tanh_part * tanh_part)).astype(BF16)
    e_gate = (vector * tanh_part * gate_part * (1.0 - gate_part)).astype(BF16)
    path = dot(e_tanh, att_tanh, ((1,), (1,))) + dot(e_gate, att_gate, ((1,), (1,)))
    dy_a = ((share * (class0 - class1) + slope * path) * (1.0 / 16.0)).astype(BF16)
    dy_b = (share * path * (1.0 / 16.0)).astype(BF16)
    blank = jnp.zeros((2 * slots, e_tanh.shape[1]), BF16)
    path_t = dot(att_tanh, jnp.concatenate([e_tanh, blank, e_tanh], axis=0), ((1,), (1,))) + dot(
        att_gate, jnp.concatenate([e_gate, blank, e_gate], axis=0), ((1,), (1,))
    )
    store_path(path_t, keep_ref, send_ref)
    scalars = [jnp.broadcast_to(v, (1, 128)) for v in (total, mean0, mean1)]
    for out_ref, shift in ((keep_ref, 0), (send_ref, slots)):
        out_ref[CORE_SUMS : CORE_SUMS + slots, :] = sum_high[:, :128]
        out_ref[CORE_SUMS + slots : CORE_NOTE, :] = sum_high[:, 128:]
        out_ref[CORE_NOTE:, :] = note_rows(*scalars, as_row(share, shift), as_row(u0 - u1, shift))
    back = dot(jnp.concatenate([dy_a, dy_b], axis=0), w_expand, ((1,), (0,))).astype(BF16)
    back = jnp.concatenate([back[:slots], back[slots:]], axis=1)
    spread = jnp.broadcast_to(back.astype(F32)[:, None, :], (slots, 16, back.shape[1]))
    spread = spread.reshape(rows, back.shape[1])
    mask = hidden_ref[...].astype(F32) > 0
    hid = mask.shape[1]
    dhid = jnp.concatenate(
        [jnp.where(mask, spread[:, :hid], 0.0), jnp.where(mask, spread[:, hid:], 0.0)], axis=1
    ).astype(BF16)
    grad_w1 = dot(flat_ref[...], dhid, ((0,), (0,)))
    store_w1(grad_w1[:, :hid], grad_w1[:, hid:], keep_ref, send_ref)


def merge(blocks, shares, offsets):
    a = b = 0.0
    half = blocks[0].shape[0] // 2
    for share, offset, block in zip(shares, offsets, blocks):
        block_b = block[half:].astype(F32)
        a = a + share * (block[:half].astype(F32) + offset * block_b)
        b = b + share * block_b
    return a.astype(BF16), b.astype(BF16)


def core_kernel(own_ref, other_ref, *out_refs):
    in_refs = (own_ref, other_ref)
    notes = [read_note(r[CORE_NOTE:, :], 5) for r in in_refs]
    total, mean0, mean1, shares, offsets = merge_notes(notes)
    tile_share = shares[0] * notes[0][3] + shares[1] * notes[1][3]
    note = note_rows(total, mean0, mean1, tile_share, notes[0][4] + notes[1][4])
    here = lax.div(lax.axis_index("tile"), NZ * NC)
    for away, out_ref in enumerate(out_refs):
        y = lax.rem(here + away, NY)
        for z in range(NZ):
            part = pl.ds(pl.multiple_of(y * W1_ROWS + z * W1_PART, W1_PART), W1_PART)
            a, b = merge([r[part, :] for r in in_refs], shares, offsets)
            out_ref[z * W1_PART : z * W1_PART + W1_PART // 2, :] = a
            out_ref[z * W1_PART + W1_PART // 2 : (z + 1) * W1_PART, :] = b
        path = pl.ds(pl.multiple_of(CORE_PATH + y * PATH_ROWS, PATH_ROWS), PATH_ROWS)
        out_ref[W1_ROWS:Y_SUMS, :] = own_ref[path, :] + other_ref[path, :]
        for half in range(2):
            for i, r in enumerate(in_refs):
                at = Y_SUMS + (2 * half + i) * SLOTS
                out_ref[at : at + SLOTS, :] = r[CORE_SUMS + half * SLOTS : CORE_SUMS + (half + 1) * SLOTS, :]
        out_ref[Y_NOTE:, :] = note


def class_column(classifier_ref, y, core):
    span = NZ * NC * ROWS
    part = pl.ds(pl.multiple_of(y * span, span), span)
    row = classifier_ref[0:1, part] - classifier_ref[1:2, part]
    rows = jnp.concatenate(split3(row) + [jnp.zeros((5, span), F32)], axis=0).astype(BF16)
    to = lax.broadcasted_iota(jnp.int32, (PATH_ROWS, span), 0)
    at = lax.broadcasted_iota(jnp.int32, (PATH_ROWS, span), 1)
    wanted = lax.div(to, ROWS) * (NC * ROWS) + core * ROWS + lax.rem(to, ROWS)
    picked = dot((wanted == at).astype(F32).astype(BF16), rows, ((1,), (1,)))
    return picked[:, 0:1] + picked[:, 1:2] + picked[:, 2:3]


def y_kernel(in0, in1, in2, in3, classifier_ref, *refs):
    in_refs, out_refs, w2_ref = (in0, in1, in2, in3), refs[:-1], refs[-1]
    notes = [read_note(r[Y_NOTE:, :], 5) for r in in_refs]
    total, mean0, mean1, shares, offsets = merge_notes(notes)
    note = note_rows(total, mean0, mean1)
    index = lax.axis_index("tile")
    column = class_column(classifier_ref, lax.div(index, NZ * NC), lax.rem(index, NC))
    lefts, sums = [], []
    for share, member, r in zip(shares, notes, in_refs):
        path = r[W1_ROWS:Y_SUMS, :].astype(F32)
        weight = share * member[3] * (1.0 / 16.0)
        slope = weight * (member[4] - (mean0 - mean1))
        lefts.append(jnp.concatenate([weight * column + slope * path, weight * path], axis=0).astype(BF16))
        halves = [r[Y_SUMS + 2 * i * SLOTS : Y_SUMS + 2 * (i + 1) * SLOTS, :] for i in range(2)]
        sums.append(jnp.concatenate(halves, axis=1))
    w2_ref[...] = dot(jnp.concatenate(lefts, axis=1), jnp.concatenate(sums, axis=0), ((1,), (0,))).astype(BF16)
    here = lax.rem(lax.div(index, NC), NZ)
    for away, out_ref in enumerate(out_refs):
        z = lax.bitwise_xor(here, away)
        part = pl.ds(pl.multiple_of(z * W1_PART, W1_PART), W1_PART)
        a, b = merge([r[part, :] for r in in_refs], shares, offsets)
        for i, block in enumerate((a, b)):
            out_ref[i * HALF : i * HALF + HALF // 2, :] = block
            rows = pl.ds(pl.multiple_of(i * PATH_ROWS + z * ROWS, ROWS), ROWS)
            for half in range(2):
                at = i * HALF + HALF // 2 + half * ROWS
                out_ref[at : at + ROWS, :] = w2_ref[rows, half * 128 : half * 128 + 128]
        out_ref[PART:, :] = note


def z_kernel(count, in0, in1, in2, in3, target_ref, w1_ref, w2_ref, loss_ref):
    in_refs = (in0, in1, in2, in3)
    notes = [read_note(r[PART:, :], 3) for r in in_refs]
    total, mean0, mean1, shares, offsets = merge_notes(notes)
    width = mean0.shape[1]
    target0 = jnp.full((1, width), target_ref[0], F32)
    target1 = jnp.full((1, width), target_ref[1], F32)
    target_sum = target0 + target1
    share0, share1 = target0 / target_sum, target1 / target_sum
    log_partition_sum = jnp.log(jnp.exp(mean0) + jnp.exp(mean1))
    loss_ref[...] = log_partition_sum - (mean0 * share0 + mean1 * share1)
    scale = count * (jnp.exp(mean0 - log_partition_sum) - share0)
    for i, out_ref in enumerate((w1_ref, w2_ref)):
        result = 0.0
        for share, offset, r in zip(shares, offsets, in_refs):
            a = r[2 * i * ROWS : 2 * (i + 1) * ROWS, :].astype(F32)
            b = r[HALF + 2 * i * ROWS : HALF + 2 * (i + 1) * ROWS, :].astype(F32)
            result = result + share * (a + offset * b)
        result = scale * result
        out_ref[:, :width] = result[:ROWS]
        out_ref[:, width:] = result[ROWS:]


def vmem(count):
    return [pl.BlockSpec(memory_space=pltpu.VMEM)] * count


def call(kernel, out_shape, in_specs, args, name, scratch=()):
    many = isinstance(out_shape, (tuple, list))
    return pl.pallas_call(
        kernel,
        out_shape=out_shape,
        in_specs=in_specs,
        out_specs=tuple(vmem(len(out_shape))) if many else vmem(1)[0],
        scratch_shapes=list(scratch),
        compiler_params=pltpu.CompilerParams(vmem_limit_bytes=VMEM_LIMIT),
        name=name,
    )(*args)


def place(y, z, core):
    return (y * NZ + z) * NC + core


def body(
    tiles,
    w_reduce,
    w_expand,
    att_tanh,
    att_gate,
    att_vector,
    classifier,
    tile_counts,
    target_weights,
):
    slots, positions, width = tiles.shape
    rows = slots * positions
    hid = w_reduce.shape[1]
    smem = pl.BlockSpec(memory_space=pltpu.SMEM)
    hbm = pl.BlockSpec(memory_space=pltpu.HBM)
    held = [
        pltpu.with_memory_space_constraint(x, pltpu.HBM)
        for x in (
            tiles.reshape(rows, width),
            w_reduce,
            w_expand,
            att_tanh,
            att_gate,
            att_vector.reshape(1, hid),
            classifier.T,
        )
    ]
    chunk = jax.ShapeDtypeStruct((CORE_NOTE + NOTE, 128), BF16)
    keep, send = call(
        local_kernel,
        (chunk, chunk),
        [smem] + [hbm] * 7,
        (tile_counts, *held),
        "local",
        [pltpu.VMEM((rows, width), BF16)]
        + [pltpu.VMEM((width, hid), BF16)] * 4
        + [pltpu.VMEM((1, hid), F32), pltpu.VMEM((2, width), F32)]
        + [pltpu.VMEM((rows, hid), BF16), pltpu.SemaphoreType.DMA((CHUNKS + 6,))],
    )
    everyone = [(y, z, c) for y in range(NY) for z in range(NZ) for c in range(NC)]

    def move(x, dy, dz, dc):
        pairs = [
            (place(y, z, c), place((y + dy) % NY, (z + dz) % NZ, (c + dc) % NC)) for y, z, c in everyone
        ]
        return lax.ppermute(x, "tile", pairs)

    def swap(x, dy, dz):
        return lax.ppermute(x, "tile", [(place(y, z, c), place(y ^ dy, z ^ dz, c)) for y, z, c in everyone])

    other = move(send, 0, 0, 1)
    piece = jax.ShapeDtypeStruct((Y_NOTE + NOTE, 128), BF16)
    pieces = call(core_kernel, (piece,) * NY, vmem(2), (keep, other), "join_cores")
    across = [move(pieces[2], 2, 0, 0), move(pieces[1], 1, 0, 0), move(pieces[3], 3, 0, 0)]
    piece = jax.ShapeDtypeStruct((PART + NOTE, 128), BF16)
    pieces = call(
        y_kernel,
        (piece,) * NZ,
        vmem(NY + 1),
        (pieces[0], *across, classifier.T),
        "join_y",
        [pltpu.VMEM((2 * PATH_ROWS, hid), BF16)],
    )
    across = [swap(pieces[2], 0, 2), swap(pieces[3], 0, 3), swap(pieces[1], 0, 1)]
    count = float(lax.axis_size("tile") * slots // 2)
    out = jax.ShapeDtypeStruct((ROWS, hid), F32)
    grad_w1, grad_w2, loss = call(
        functools.partial(z_kernel, count),
        (out, out, jax.ShapeDtypeStruct((1, 128), F32)),
        vmem(NZ) + [smem],
        (pieces[0], *across, target_weights),
        "join_z",
    )
    return grad_w1, grad_w2, loss[0, :1]


def solution(mesh):
    placed = (
        P(("slide", "tile"), None, None),
        P(),
        P(),
        P(),
        P(),
        P(),
        P(),
        P(("slide", "tile")),
        P("slide"),
    )
    return jax.shard_map(
        body,
        mesh=mesh,
        in_specs=placed,
        out_specs=(P(("slide", "tile"), None), P(("slide", "tile"), None), P("slide")),
        check_vma=False,
    )
```

```python
import functools

import jax
import jax.numpy as jnp
from jax import lax
from jax.experimental import pallas as pl
from jax.experimental.pallas import tpu as pltpu
from jax.sharding import PartitionSpec as P

F32 = jnp.float32
BF16 = jnp.bfloat16
NY, NZ, NC = 4, 4, 2
ROWS = 32
PART = 8 * ROWS
HALF = PART // 2
W1_PART = 4 * ROWS
W1_ROWS = NZ * W1_PART
PATH_ROWS = NZ * ROWS
SLOTS = 64
CORE_PATH = NY * W1_ROWS
CORE_SUMS = CORE_PATH + NY * PATH_ROWS
CORE_NOTE = CORE_SUMS + 2 * SLOTS
Y_SUMS = W1_ROWS + PATH_ROWS
Y_NOTE = Y_SUMS + 4 * SLOTS
NOTE = 16
VMEM_LIMIT = 48 * 1024 * 1024


def dot(a, b, dims):
    return lax.dot_general(a, b, (dims, ((), ())), preferred_element_type=F32)


def split3(x):
    high = x.astype(BF16)
    rest = x - high.astype(F32)
    mid = rest.astype(BF16)
    low = (rest - mid.astype(F32)).astype(BF16)
    return [high.astype(F32), mid.astype(F32), low.astype(F32)]


def note_rows(*values):
    rows = [part for value in values for part in split3(value)]
    if len(rows) < NOTE:
        rows.append(jnp.zeros((NOTE - len(rows), rows[0].shape[1]), F32))
    return jnp.concatenate(rows, axis=0).astype(BF16)


def read_note(note, count):
    rows = note.astype(F32)
    return [
        rows[i : i + 1] + rows[i + 1 : i + 2] + rows[i + 2 : i + 3] for i in range(0, 3 * count, 3)
    ]


def merge_notes(notes):
    total = sum(n[0] for n in notes)
    shares = [n[0] / total for n in notes]
    mean0 = sum(a * n[1] for a, n in zip(shares, notes))
    mean1 = sum(a * n[2] for a, n in zip(shares, notes))
    offsets = [(n[1] - n[2]) - (mean0 - mean1) for n in notes]
    return total, mean0, mean1, shares, offsets


def position_sum(x):
    return jnp.sum(x.reshape(x.shape[0] // 16, 16, x.shape[1]).astype(F32), axis=1)


def store_w1(part_a, part_b, keep_ref, send_ref):
    first = lax.rem(lax.axis_index("tile"), NC) == 0
    for y in range(NY):
        for z in range(NZ):
            at = (y * NZ + z) * NC * ROWS
            for i, part in enumerate((part_a, part_b)):
                for half in range(2):
                    cols = slice(half * 128, half * 128 + 128)
                    even = part[at : at + ROWS, cols].astype(BF16)
                    odd = part[at + ROWS : at + 2 * ROWS, cols].astype(BF16)
                    here = pl.ds(y * W1_ROWS + z * W1_PART + (2 * i + half) * ROWS, ROWS)
                    keep_ref[here, :] = jnp.where(first, even, odd)
                    send_ref[here, :] = jnp.where(first, odd, even)


def store_path(path, keep_ref, send_ref):
    first = lax.rem(lax.axis_index("tile"), NC) == 0
    for k in range(NY * NZ):
        at = k * NC * ROWS
        even, odd = path[at : at + ROWS], path[at + ROWS : at + 2 * ROWS]
        here = pl.ds(CORE_PATH + k * ROWS, ROWS)
        keep_ref[here, :] = jnp.where(first, even[:, :128], odd[:, :128]).astype(BF16)
        send_ref[here, :] = jnp.where(first, odd[:, 128:], even[:, 128:]).astype(BF16)


def as_row(column, shift):
    slot = lax.broadcasted_iota(jnp.int32, (column.shape[0], 128), 0)
    lane = lax.broadcasted_iota(jnp.int32, (column.shape[0], 128), 1)
    return jnp.sum(jnp.where(slot + shift == lane, column, 0.0), axis=0, keepdims=True)


CHUNKS = 2


def local_kernel(
    count_ref,
    tiles_hbm,
    w_reduce_hbm,
    w_expand_hbm,
    att_tanh_hbm,
    att_gate_hbm,
    att_vector_hbm,
    classifier_hbm,
    keep_ref,
    send_ref,
    flat_ref,
    w_reduce_ref,
    w_expand_ref,
    att_tanh_ref,
    att_gate_ref,
    att_vector_ref,
    classifier_ref,
    hidden_ref,
    sem,
):
    rows, width = flat_ref.shape
    slots = rows // 16
    step = rows // CHUNKS
    copies = [pltpu.make_async_copy(w_reduce_hbm, w_reduce_ref, sem.at[CHUNKS])]
    for i in range(CHUNKS):
        part = pl.ds(i * step, step)
        copies.append(pltpu.make_async_copy(tiles_hbm.at[part], flat_ref.at[part], sem.at[i]))
    copies.append(pltpu.make_async_copy(w_expand_hbm, w_expand_ref, sem.at[CHUNKS + 1]))
    copies.append(pltpu.make_async_copy(att_tanh_hbm, att_tanh_ref, sem.at[CHUNKS + 2]))
    copies.append(pltpu.make_async_copy(att_gate_hbm, att_gate_ref, sem.at[CHUNKS + 3]))
    copies.append(pltpu.make_async_copy(att_vector_hbm, att_vector_ref, sem.at[CHUNKS + 4]))
    copies.append(pltpu.make_async_copy(classifier_hbm, classifier_ref, sem.at[CHUNKS + 5]))
    for copy in copies:
        copy.start()
    copies[0].wait()
    w_reduce = w_reduce_ref[...]
    tile_sums, hidden_sums = [], []
    for i in range(CHUNKS):
        copies[1 + i].wait()
        part = pl.ds(i * step, step)
        flat = flat_ref[part, :]
        hidden = jnp.maximum(dot(flat, w_reduce, ((1,), (0,))), 0.0).astype(BF16)
        hidden_ref[part, :] = hidden
        tile_sums.append(position_sum(flat))
        hidden_sums.append(position_sum(hidden))
    tile_sum = jnp.concatenate(tile_sums, axis=0)
    hidden_sum = jnp.concatenate(hidden_sums, axis=0)
    sum_high = hidden_sum.astype(BF16)
    sum_low = (hidden_sum - sum_high.astype(F32)).astype(BF16)
    copies[CHUNKS + 1].wait()
    w_expand = w_expand_ref[...]
    sums = jnp.concatenate([sum_high, sum_low], axis=0)
    expanded = dot(sums, w_expand, ((1,), (1,)))
    embed = ((tile_sum + expanded[:slots] + expanded[slots:]) * (1.0 / 16.0)).astype(BF16)
    for copy in copies[CHUNKS + 2 :]:
        copy.wait()
    att_tanh, att_gate = att_tanh_ref[...], att_gate_ref[...]
    tanh_part = jnp.tanh(dot(embed, att_tanh, ((1,), (0,))))
    gate_part = jax.nn.sigmoid(dot(embed, att_gate, ((1,), (0,))))
    vector = att_vector_ref[...]
    score = jnp.sum(tanh_part * gate_part * vector, axis=1, keepdims=True)
    slot = lax.broadcasted_iota(jnp.int32, (slots, 1), 0)
    weight = jnp.where(slot < count_ref[0], jnp.exp(score), 0.0)
    total = jnp.sum(weight, axis=0, keepdims=True)
    share = weight / total
    embed_float = embed.astype(F32)
    class0, class1 = classifier_ref[0:1, :], classifier_ref[1:2, :]
    u0 = jnp.sum(embed_float * class0, axis=1, keepdims=True)
    u1 = jnp.sum(embed_float * class1, axis=1, keepdims=True)
    mean0 = jnp.sum(share * u0, axis=0, keepdims=True)
    mean1 = jnp.sum(share * u1, axis=0, keepdims=True)
    slope = share * ((u0 - u1) - (mean0 - mean1))
    e_tanh = (vector * gate_part * (1.0 - tanh_part * tanh_part)).astype(BF16)
    e_gate = (vector * tanh_part * gate_part * (1.0 - gate_part)).astype(BF16)
    path = dot(e_tanh, att_tanh, ((1,), (1,))) + dot(e_gate, att_gate, ((1,), (1,)))
    dy_a = ((share * (class0 - class1) + slope * path) * (1.0 / 16.0)).astype(BF16)
    dy_b = (share * path * (1.0 / 16.0)).astype(BF16)
    blank = jnp.zeros((2 * slots, e_tanh.shape[1]), BF16)
    path_t = dot(att_tanh, jnp.concatenate([e_tanh, blank, e_tanh], axis=0), ((1,), (1,))) + dot(
        att_gate, jnp.concatenate([e_gate, blank, e_gate], axis=0), ((1,), (1,))
    )
    store_path(path_t, keep_ref, send_ref)
    scalars = [jnp.broadcast_to(v, (1, 128)) for v in (total, mean0, mean1)]
    for out_ref, shift in ((keep_ref, 0), (send_ref, slots)):
        out_ref[CORE_SUMS : CORE_SUMS + slots, :] = sum_high[:, :128]
        out_ref[CORE_SUMS + slots : CORE_NOTE, :] = sum_high[:, 128:]
        out_ref[CORE_NOTE:, :] = note_rows(*scalars, as_row(share, shift), as_row(u0 - u1, shift))
    back = dot(jnp.concatenate([dy_a, dy_b], axis=0), w_expand, ((1,), (0,))).astype(BF16)
    back = jnp.concatenate([back[:slots], back[slots:]], axis=1)
    spread = jnp.broadcast_to(back.astype(F32)[:, None, :], (slots, 16, back.shape[1]))
    spread = spread.reshape(rows, back.shape[1])
    mask = hidden_ref[...].astype(F32) > 0
    hid = mask.shape[1]
    dhid = jnp.concatenate(
        [jnp.where(mask, spread[:, :hid], 0.0), jnp.where(mask, spread[:, hid:], 0.0)], axis=1
    ).astype(BF16)
    grad_w1 = dot(flat_ref[...], dhid, ((0,), (0,)))
    store_w1(grad_w1[:, :hid], grad_w1[:, hid:], keep_ref, send_ref)


def merge(blocks, shares, offsets):
    a = b = 0.0
    half = blocks[0].shape[0] // 2
    for share, offset, block in zip(shares, offsets, blocks):
        block_b = block[half:].astype(F32)
        a = a + share * (block[:half].astype(F32) + offset * block_b)
        b = b + share * block_b
    return a.astype(BF16), b.astype(BF16)


def core_kernel(own_ref, other_ref, *out_refs):
    in_refs = (own_ref, other_ref)
    notes = [read_note(r[CORE_NOTE:, :], 5) for r in in_refs]
    total, mean0, mean1, shares, offsets = merge_notes(notes)
    tile_share = shares[0] * notes[0][3] + shares[1] * notes[1][3]
    note = note_rows(total, mean0, mean1, tile_share, notes[0][4] + notes[1][4])
    here = lax.div(lax.axis_index("tile"), NZ * NC)
    for away, out_ref in enumerate(out_refs):
        y = lax.rem(here + away, NY)
        for z in range(NZ):
            part = pl.ds(pl.multiple_of(y * W1_ROWS + z * W1_PART, W1_PART), W1_PART)
            a, b = merge([r[part, :] for r in in_refs], shares, offsets)
            out_ref[z * W1_PART : z * W1_PART + W1_PART // 2, :] = a
            out_ref[z * W1_PART + W1_PART // 2 : (z + 1) * W1_PART, :] = b
        path = pl.ds(pl.multiple_of(CORE_PATH + y * PATH_ROWS, PATH_ROWS), PATH_ROWS)
        out_ref[W1_ROWS:Y_SUMS, :] = own_ref[path, :] + other_ref[path, :]
        for half in range(2):
            for i, r in enumerate(in_refs):
                at = Y_SUMS + (2 * half + i) * SLOTS
                out_ref[at : at + SLOTS, :] = r[CORE_SUMS + half * SLOTS : CORE_SUMS + (half + 1) * SLOTS, :]
        out_ref[Y_NOTE:, :] = note


def class_column(classifier_ref, y, core):
    span = NZ * NC * ROWS
    part = pl.ds(pl.multiple_of(y * span, span), span)
    row = classifier_ref[0:1, part] - classifier_ref[1:2, part]
    rows = jnp.concatenate(split3(row) + [jnp.zeros((5, span), F32)], axis=0).astype(BF16)
    to = lax.broadcasted_iota(jnp.int32, (PATH_ROWS, span), 0)
    at = lax.broadcasted_iota(jnp.int32, (PATH_ROWS, span), 1)
    wanted = lax.div(to, ROWS) * (NC * ROWS) + core * ROWS + lax.rem(to, ROWS)
    picked = dot((wanted == at).astype(F32).astype(BF16), rows, ((1,), (1,)))
    return picked[:, 0:1] + picked[:, 1:2] + picked[:, 2:3]


Z_AWAY = ((2, 3, 1), (2, 1, 3))


def y_kernel(in0, in1, in2, in3, classifier_ref, *refs):
    in_refs, out_refs, w2_ref = (in0, in1, in2, in3), refs[:-1], refs[-1]
    notes = [read_note(r[Y_NOTE:, :], 5) for r in in_refs]
    total, mean0, mean1, shares, offsets = merge_notes(notes)
    note = note_rows(total, mean0, mean1)
    index = lax.axis_index("tile")
    column = class_column(classifier_ref, lax.div(index, NZ * NC), lax.rem(index, NC))
    lefts, sums = [], []
    for share, member, r in zip(shares, notes, in_refs):
        path = r[W1_ROWS:Y_SUMS, :].astype(F32)
        weight = share * member[3] * (1.0 / 16.0)
        slope = weight * (member[4] - (mean0 - mean1))
        lefts.append(jnp.concatenate([weight * column + slope * path, weight * path], axis=0).astype(BF16))
        halves = [r[Y_SUMS + 2 * i * SLOTS : Y_SUMS + 2 * (i + 1) * SLOTS, :] for i in range(2)]
        sums.append(jnp.concatenate(halves, axis=1))
    w2_ref[...] = dot(jnp.concatenate(lefts, axis=1), jnp.concatenate(sums, axis=0), ((1,), (0,))).astype(BF16)
    here = lax.rem(lax.div(index, NC), NZ)
    odd = lax.rem(index, NC)
    for even_away, odd_away, out_ref in zip((0, *Z_AWAY[0]), (0, *Z_AWAY[1]), out_refs):
        z = lax.bitwise_xor(here, even_away + odd * (odd_away - even_away))
        part = pl.ds(pl.multiple_of(z * W1_PART, W1_PART), W1_PART)
        a, b = merge([r[part, :] for r in in_refs], shares, offsets)
        for i, block in enumerate((a, b)):
            out_ref[i * HALF : i * HALF + HALF // 2, :] = block
            rows = pl.ds(pl.multiple_of(i * PATH_ROWS + z * ROWS, ROWS), ROWS)
            for half in range(2):
                at = i * HALF + HALF // 2 + half * ROWS
                out_ref[at : at + ROWS, :] = w2_ref[rows, half * 128 : half * 128 + 128]
        out_ref[PART:, :] = note


def z_kernel(count, in0, in1, in2, in3, target_ref, w1_ref, w2_ref, loss_ref):
    in_refs = (in0, in1, in2, in3)
    notes = [read_note(r[PART:, :], 3) for r in in_refs]
    total, mean0, mean1, shares, offsets = merge_notes(notes)
    width = mean0.shape[1]
    target0 = jnp.full((1, width), target_ref[0], F32)
    target1 = jnp.full((1, width), target_ref[1], F32)
    target_sum = target0 + target1
    share0, share1 = target0 / target_sum, target1 / target_sum
    log_partition_sum = jnp.log(jnp.exp(mean0) + jnp.exp(mean1))
    loss_ref[...] = log_partition_sum - (mean0 * share0 + mean1 * share1)
    scale = count * (jnp.exp(mean0 - log_partition_sum) - share0)
    for i, out_ref in enumerate((w1_ref, w2_ref)):
        result = 0.0
        for share, offset, r in zip(shares, offsets, in_refs):
            a = r[2 * i * ROWS : 2 * (i + 1) * ROWS, :].astype(F32)
            b = r[HALF + 2 * i * ROWS : HALF + 2 * (i + 1) * ROWS, :].astype(F32)
            result = result + share * (a + offset * b)
        result = scale * result
        out_ref[:, :width] = result[:ROWS]
        out_ref[:, width:] = result[ROWS:]


def vmem(count):
    return [pl.BlockSpec(memory_space=pltpu.VMEM)] * count


def call(kernel, out_shape, in_specs, args, name, scratch=()):
    many = isinstance(out_shape, (tuple, list))
    return pl.pallas_call(
        kernel,
        out_shape=out_shape,
        in_specs=in_specs,
        out_specs=tuple(vmem(len(out_shape))) if many else vmem(1)[0],
        scratch_shapes=list(scratch),
        compiler_params=pltpu.CompilerParams(vmem_limit_bytes=VMEM_LIMIT),
        name=name,
    )(*args)


def place(y, z, core):
    return (y * NZ + z) * NC + core


def body(
    tiles,
    w_reduce,
    w_expand,
    att_tanh,
    att_gate,
    att_vector,
    classifier,
    tile_counts,
    target_weights,
):
    slots, positions, width = tiles.shape
    rows = slots * positions
    hid = w_reduce.shape[1]
    smem = pl.BlockSpec(memory_space=pltpu.SMEM)
    hbm = pl.BlockSpec(memory_space=pltpu.HBM)
    held = [
        pltpu.with_memory_space_constraint(x, pltpu.HBM)
        for x in (
            tiles.reshape(rows, width),
            w_reduce,
            w_expand,
            att_tanh,
            att_gate,
            att_vector.reshape(1, hid),
            classifier.T,
        )
    ]
    chunk = jax.ShapeDtypeStruct((CORE_NOTE + NOTE, 128), BF16)
    keep, send = call(
        local_kernel,
        (chunk, chunk),
        [smem] + [hbm] * 7,
        (tile_counts, *held),
        "local",
        [pltpu.VMEM((rows, width), BF16)]
        + [pltpu.VMEM((width, hid), BF16)] * 4
        + [pltpu.VMEM((1, hid), F32), pltpu.VMEM((2, width), F32)]
        + [pltpu.VMEM((rows, hid), BF16), pltpu.SemaphoreType.DMA((CHUNKS + 6,))],
    )
    everyone = [(y, z, c) for y in range(NY) for z in range(NZ) for c in range(NC)]

    def move(x, dy, dz, dc):
        pairs = [
            (place(y, z, c), place((y + dy) % NY, (z + dz) % NZ, (c + dc) % NC)) for y, z, c in everyone
        ]
        return lax.ppermute(x, "tile", pairs)

    def swap(x, away):
        return lax.ppermute(x, "tile", [(place(y, z, c), place(y, z ^ away[c], c)) for y, z, c in everyone])

    other = move(send, 0, 0, 1)
    piece = jax.ShapeDtypeStruct((Y_NOTE + NOTE, 128), BF16)
    pieces = call(core_kernel, (piece,) * NY, vmem(2), (keep, other), "join_cores")
    across = [move(pieces[2], 2, 0, 0), move(pieces[1], 1, 0, 0), move(pieces[3], 3, 0, 0)]
    piece = jax.ShapeDtypeStruct((PART + NOTE, 128), BF16)
    pieces = call(
        y_kernel,
        (piece,) * NZ,
        vmem(NY + 1),
        (pieces[0], *across, classifier.T),
        "join_y",
        [pltpu.VMEM((2 * PATH_ROWS, hid), BF16)],
    )
    across = [swap(pieces[k + 1], [away[k] for away in Z_AWAY]) for k in range(NZ - 1)]
    count = float(lax.axis_size("tile") * slots // 2)
    out = jax.ShapeDtypeStruct((ROWS, hid), F32)
    grad_w1, grad_w2, loss = call(
        functools.partial(z_kernel, count),
        (out, out, jax.ShapeDtypeStruct((1, 128), F32)),
        vmem(NZ) + [smem],
        (pieces[0], *across, target_weights),
        "join_z",
    )
    return grad_w1, grad_w2, loss[0, :1]


def solution(mesh):
    placed = (
        P(("slide", "tile"), None, None),
        P(),
        P(),
        P(),
        P(),
        P(),
        P(),
        P(("slide", "tile")),
        P("slide"),
    )
    return jax.shard_map(
        body,
        mesh=mesh,
        in_specs=placed,
        out_specs=(P(("slide", "tile"), None), P(("slide", "tile"), None), P("slide")),
        check_vma=False,
    )
```

```python
import functools

import jax
import jax.numpy as jnp
from jax import lax
from jax.experimental import pallas as pl
from jax.experimental.pallas import tpu as pltpu
from jax.sharding import PartitionSpec as P

F32 = jnp.float32
BF16 = jnp.bfloat16
NY, NZ, NC = 4, 4, 2
ROWS = 32
PART = 8 * ROWS
HALF = PART // 2
W1_PART = 4 * ROWS
W1_ROWS = NZ * W1_PART
PATH_ROWS = NZ * ROWS
SLOTS = 64
CORE_PATH = NY * W1_ROWS
CORE_SUMS = CORE_PATH + NY * PATH_ROWS
CORE_NOTE = CORE_SUMS + 2 * SLOTS
Y_SUMS = W1_ROWS + PATH_ROWS
Y_NOTE = Y_SUMS + 4 * SLOTS
NOTE = 16
VMEM_LIMIT = 48 * 1024 * 1024


def dot(a, b, dims):
    return lax.dot_general(a, b, (dims, ((), ())), preferred_element_type=F32)


def split3(x):
    high = x.astype(BF16)
    rest = x - high.astype(F32)
    mid = rest.astype(BF16)
    low = (rest - mid.astype(F32)).astype(BF16)
    return [high.astype(F32), mid.astype(F32), low.astype(F32)]


def note_rows(*values):
    rows = [part for value in values for part in split3(value)]
    if len(rows) < NOTE:
        rows.append(jnp.zeros((NOTE - len(rows), rows[0].shape[1]), F32))
    return jnp.concatenate(rows, axis=0).astype(BF16)


def read_note(note, count):
    rows = note.astype(F32)
    return [
        rows[i : i + 1] + rows[i + 1 : i + 2] + rows[i + 2 : i + 3] for i in range(0, 3 * count, 3)
    ]


def merge_notes(notes):
    total = sum(n[0] for n in notes)
    shares = [n[0] / total for n in notes]
    mean0 = sum(a * n[1] for a, n in zip(shares, notes))
    mean1 = sum(a * n[2] for a, n in zip(shares, notes))
    offsets = [(n[1] - n[2]) - (mean0 - mean1) for n in notes]
    return total, mean0, mean1, shares, offsets


def position_sum(x):
    return jnp.sum(x.reshape(x.shape[0] // 16, 16, x.shape[1]).astype(F32), axis=1)


def store_w1(part_a, part_b, keep_ref, send_ref):
    first = lax.rem(lax.axis_index("tile"), NC) == 0
    for y in range(NY):
        for z in range(NZ):
            at = (y * NZ + z) * NC * ROWS
            for i, part in enumerate((part_a, part_b)):
                for half in range(2):
                    cols = slice(half * 128, half * 128 + 128)
                    even = part[at : at + ROWS, cols].astype(BF16)
                    odd = part[at + ROWS : at + 2 * ROWS, cols].astype(BF16)
                    here = pl.ds(y * W1_ROWS + z * W1_PART + (2 * i + half) * ROWS, ROWS)
                    keep_ref[here, :] = jnp.where(first, even, odd)
                    send_ref[here, :] = jnp.where(first, odd, even)


def store_path(path, keep_ref, send_ref):
    first = lax.rem(lax.axis_index("tile"), NC) == 0
    own = lax.broadcasted_iota(jnp.int32, (ROWS, 2 * SLOTS), 1) < SLOTS
    for k in range(NY * NZ):
        at = k * NC * ROWS
        even, odd = path[at : at + ROWS], path[at + ROWS : at + 2 * ROWS]
        here = pl.ds(CORE_PATH + k * ROWS, ROWS)
        keep_ref[here, :] = jnp.where(own, jnp.where(first, even, odd), 0.0).astype(BF16)
        send_ref[here, :] = jnp.where(own, 0.0, jnp.where(first, odd, even)).astype(BF16)


def as_row(column, shift):
    slot = lax.broadcasted_iota(jnp.int32, (column.shape[0], 128), 0)
    lane = lax.broadcasted_iota(jnp.int32, (column.shape[0], 128), 1)
    return jnp.sum(jnp.where(slot + shift == lane, column, 0.0), axis=0, keepdims=True)


CHUNKS = 2


def local_kernel(
    count_ref,
    tiles_hbm,
    w_reduce_hbm,
    w_expand_hbm,
    att_tanh_hbm,
    att_gate_hbm,
    att_vector_hbm,
    classifier_hbm,
    keep_ref,
    send_ref,
    flat_ref,
    w_reduce_ref,
    w_expand_ref,
    att_tanh_ref,
    att_gate_ref,
    att_vector_ref,
    classifier_ref,
    hidden_ref,
    sem,
):
    rows, width = flat_ref.shape
    slots = rows // 16
    step = rows // CHUNKS
    copies = [pltpu.make_async_copy(w_reduce_hbm, w_reduce_ref, sem.at[CHUNKS])]
    for i in range(CHUNKS):
        part = pl.ds(i * step, step)
        copies.append(pltpu.make_async_copy(tiles_hbm.at[part], flat_ref.at[part], sem.at[i]))
    copies.append(pltpu.make_async_copy(w_expand_hbm, w_expand_ref, sem.at[CHUNKS + 1]))
    copies.append(pltpu.make_async_copy(att_tanh_hbm, att_tanh_ref, sem.at[CHUNKS + 2]))
    copies.append(pltpu.make_async_copy(att_gate_hbm, att_gate_ref, sem.at[CHUNKS + 3]))
    copies.append(pltpu.make_async_copy(att_vector_hbm, att_vector_ref, sem.at[CHUNKS + 4]))
    copies.append(pltpu.make_async_copy(classifier_hbm, classifier_ref, sem.at[CHUNKS + 5]))
    for copy in copies:
        copy.start()
    copies[0].wait()
    w_reduce = w_reduce_ref[...]
    tile_sums, hidden_sums = [], []
    for i in range(CHUNKS):
        copies[1 + i].wait()
        part = pl.ds(i * step, step)
        flat = flat_ref[part, :]
        hidden = jnp.maximum(dot(flat, w_reduce, ((1,), (0,))), 0.0).astype(BF16)
        hidden_ref[part, :] = hidden
        tile_sums.append(position_sum(flat))
        hidden_sums.append(position_sum(hidden))
    tile_sum = jnp.concatenate(tile_sums, axis=0)
    hidden_sum = jnp.concatenate(hidden_sums, axis=0)
    sum_high = hidden_sum.astype(BF16)
    sum_low = (hidden_sum - sum_high.astype(F32)).astype(BF16)
    copies[CHUNKS + 1].wait()
    w_expand = w_expand_ref[...]
    sums = jnp.concatenate([sum_high, sum_low], axis=0)
    expanded = dot(sums, w_expand, ((1,), (1,)))
    embed = ((tile_sum + expanded[:slots] + expanded[slots:]) * (1.0 / 16.0)).astype(BF16)
    for copy in copies[CHUNKS + 2 :]:
        copy.wait()
    att_tanh, att_gate = att_tanh_ref[...], att_gate_ref[...]
    tanh_part = jnp.tanh(dot(embed, att_tanh, ((1,), (0,))))
    gate_part = jax.nn.sigmoid(dot(embed, att_gate, ((1,), (0,))))
    vector = att_vector_ref[...]
    score = jnp.sum(tanh_part * gate_part * vector, axis=1, keepdims=True)
    slot = lax.broadcasted_iota(jnp.int32, (slots, 1), 0)
    weight = jnp.where(slot < count_ref[0], jnp.exp(score), 0.0)
    total = jnp.sum(weight, axis=0, keepdims=True)
    share = weight / total
    embed_float = embed.astype(F32)
    class0, class1 = classifier_ref[0:1, :], classifier_ref[1:2, :]
    u0 = jnp.sum(embed_float * class0, axis=1, keepdims=True)
    u1 = jnp.sum(embed_float * class1, axis=1, keepdims=True)
    mean0 = jnp.sum(share * u0, axis=0, keepdims=True)
    mean1 = jnp.sum(share * u1, axis=0, keepdims=True)
    slope = share * ((u0 - u1) - (mean0 - mean1))
    e_tanh = (vector * gate_part * (1.0 - tanh_part * tanh_part)).astype(BF16)
    e_gate = (vector * tanh_part * gate_part * (1.0 - gate_part)).astype(BF16)
    path = dot(e_tanh, att_tanh, ((1,), (1,))) + dot(e_gate, att_gate, ((1,), (1,)))
    dy_a = ((share * (class0 - class1) + slope * path) * (1.0 / 16.0)).astype(BF16)
    dy_b = (share * path * (1.0 / 16.0)).astype(BF16)
    path_t = dot(att_tanh, jnp.concatenate([e_tanh, e_tanh], axis=0), ((1,), (1,))) + dot(
        att_gate, jnp.concatenate([e_gate, e_gate], axis=0), ((1,), (1,))
    )
    store_path(path_t, keep_ref, send_ref)
    scalars = [jnp.broadcast_to(v, (1, 128)) for v in (total, mean0, mean1)]
    for out_ref, shift in ((keep_ref, 0), (send_ref, slots)):
        out_ref[CORE_SUMS : CORE_SUMS + slots, :] = sum_high[:, :128]
        out_ref[CORE_SUMS + slots : CORE_NOTE, :] = sum_high[:, 128:]
        out_ref[CORE_NOTE:, :] = note_rows(*scalars, as_row(share, shift), as_row(u0 - u1, shift))
    back = dot(jnp.concatenate([dy_a, dy_b], axis=0), w_expand, ((1,), (0,))).astype(BF16)
    back = jnp.concatenate([back[:slots], back[slots:]], axis=1)
    spread = jnp.broadcast_to(back.astype(F32)[:, None, :], (slots, 16, back.shape[1]))
    spread = spread.reshape(rows, back.shape[1])
    mask = hidden_ref[...].astype(F32) > 0
    hid = mask.shape[1]
    dhid = jnp.concatenate(
        [jnp.where(mask, spread[:, :hid], 0.0), jnp.where(mask, spread[:, hid:], 0.0)], axis=1
    ).astype(BF16)
    grad_w1 = dot(flat_ref[...], dhid, ((0,), (0,)))
    store_w1(grad_w1[:, :hid], grad_w1[:, hid:], keep_ref, send_ref)


def merge(blocks, shares, offsets):
    a = b = 0.0
    half = blocks[0].shape[0] // 2
    for share, offset, block in zip(shares, offsets, blocks):
        block_b = block[half:].astype(F32)
        a = a + share * (block[:half].astype(F32) + offset * block_b)
        b = b + share * block_b
    return a.astype(BF16), b.astype(BF16)


def core_kernel(own_ref, other_ref, *out_refs):
    in_refs = (own_ref, other_ref)
    notes = [read_note(r[CORE_NOTE:, :], 5) for r in in_refs]
    total, mean0, mean1, shares, offsets = merge_notes(notes)
    tile_share = shares[0] * notes[0][3] + shares[1] * notes[1][3]
    note = note_rows(total, mean0, mean1, tile_share, notes[0][4] + notes[1][4])
    here = lax.div(lax.axis_index("tile"), NZ * NC)
    for away, out_ref in enumerate(out_refs):
        y = lax.rem(here + away, NY)
        for z in range(NZ):
            part = pl.ds(pl.multiple_of(y * W1_ROWS + z * W1_PART, W1_PART), W1_PART)
            a, b = merge([r[part, :] for r in in_refs], shares, offsets)
            out_ref[z * W1_PART : z * W1_PART + W1_PART // 2, :] = a
            out_ref[z * W1_PART + W1_PART // 2 : (z + 1) * W1_PART, :] = b
        path = pl.ds(pl.multiple_of(CORE_PATH + y * PATH_ROWS, PATH_ROWS), PATH_ROWS)
        out_ref[W1_ROWS:Y_SUMS, :] = own_ref[path, :] + other_ref[path, :]
        for half in range(2):
            for i, r in enumerate(in_refs):
                at = Y_SUMS + (2 * half + i) * SLOTS
                out_ref[at : at + SLOTS, :] = r[CORE_SUMS + half * SLOTS : CORE_SUMS + (half + 1) * SLOTS, :]
        out_ref[Y_NOTE:, :] = note


def class_column(classifier_ref, y, core):
    span = NZ * NC * ROWS
    part = pl.ds(pl.multiple_of(y * span, span), span)
    row = classifier_ref[0:1, part] - classifier_ref[1:2, part]
    rows = jnp.concatenate(split3(row) + [jnp.zeros((5, span), F32)], axis=0).astype(BF16)
    to = lax.broadcasted_iota(jnp.int32, (PATH_ROWS, span), 0)
    at = lax.broadcasted_iota(jnp.int32, (PATH_ROWS, span), 1)
    wanted = lax.div(to, ROWS) * (NC * ROWS) + core * ROWS + lax.rem(to, ROWS)
    picked = dot((wanted == at).astype(F32).astype(BF16), rows, ((1,), (1,)))
    return picked[:, 0:1] + picked[:, 1:2] + picked[:, 2:3]


Z_AWAY = ((2, 3, 1), (2, 1, 3))


def y_kernel(in0, in1, in2, in3, classifier_ref, *refs):
    in_refs, out_refs, w2_ref = (in0, in1, in2, in3), refs[:-1], refs[-1]
    notes = [read_note(r[Y_NOTE:, :], 5) for r in in_refs]
    total, mean0, mean1, shares, offsets = merge_notes(notes)
    note = note_rows(total, mean0, mean1)
    index = lax.axis_index("tile")
    column = class_column(classifier_ref, lax.div(index, NZ * NC), lax.rem(index, NC))
    lefts, sums = [], []
    for share, member, r in zip(shares, notes, in_refs):
        path = r[W1_ROWS:Y_SUMS, :].astype(F32)
        weight = share * member[3] * (1.0 / 16.0)
        slope = weight * (member[4] - (mean0 - mean1))
        lefts.append(jnp.concatenate([weight * column + slope * path, weight * path], axis=0).astype(BF16))
        halves = [r[Y_SUMS + 2 * i * SLOTS : Y_SUMS + 2 * (i + 1) * SLOTS, :] for i in range(2)]
        sums.append(jnp.concatenate(halves, axis=1))
    w2_ref[...] = dot(jnp.concatenate(lefts, axis=1), jnp.concatenate(sums, axis=0), ((1,), (0,))).astype(BF16)
    here = lax.rem(lax.div(index, NC), NZ)
    odd = lax.rem(index, NC)
    for even_away, odd_away, out_ref in zip((0, *Z_AWAY[0]), (0, *Z_AWAY[1]), out_refs):
        z = lax.bitwise_xor(here, even_away + odd * (odd_away - even_away))
        part = pl.ds(pl.multiple_of(z * W1_PART, W1_PART), W1_PART)
        a, b = merge([r[part, :] for r in in_refs], shares, offsets)
        for i, block in enumerate((a, b)):
            out_ref[i * HALF : i * HALF + HALF // 2, :] = block
            rows = pl.ds(pl.multiple_of(i * PATH_ROWS + z * ROWS, ROWS), ROWS)
            for half in range(2):
                at = i * HALF + HALF // 2 + half * ROWS
                out_ref[at : at + ROWS, :] = w2_ref[rows, half * 128 : half * 128 + 128]
        out_ref[PART:, :] = note


def z_kernel(count, in0, in1, in2, in3, target_ref, w1_ref, w2_ref, loss_ref):
    in_refs = (in0, in1, in2, in3)
    notes = [read_note(r[PART:, :], 3) for r in in_refs]
    total, mean0, mean1, shares, offsets = merge_notes(notes)
    width = mean0.shape[1]
    target0 = jnp.full((1, width), target_ref[0], F32)
    target1 = jnp.full((1, width), target_ref[1], F32)
    target_sum = target0 + target1
    share0, share1 = target0 / target_sum, target1 / target_sum
    log_partition_sum = jnp.log(jnp.exp(mean0) + jnp.exp(mean1))
    loss_ref[...] = log_partition_sum - (mean0 * share0 + mean1 * share1)
    scale = count * (jnp.exp(mean0 - log_partition_sum) - share0)
    for i, out_ref in enumerate((w1_ref, w2_ref)):
        result = 0.0
        for share, offset, r in zip(shares, offsets, in_refs):
            a = r[2 * i * ROWS : 2 * (i + 1) * ROWS, :].astype(F32)
            b = r[HALF + 2 * i * ROWS : HALF + 2 * (i + 1) * ROWS, :].astype(F32)
            result = result + share * (a + offset * b)
        result = scale * result
        out_ref[:, :width] = result[:ROWS]
        out_ref[:, width:] = result[ROWS:]


def vmem(count):
    return [pl.BlockSpec(memory_space=pltpu.VMEM)] * count


def call(kernel, out_shape, in_specs, args, name, scratch=()):
    many = isinstance(out_shape, (tuple, list))
    return pl.pallas_call(
        kernel,
        out_shape=out_shape,
        in_specs=in_specs,
        out_specs=tuple(vmem(len(out_shape))) if many else vmem(1)[0],
        scratch_shapes=list(scratch),
        compiler_params=pltpu.CompilerParams(vmem_limit_bytes=VMEM_LIMIT),
        name=name,
    )(*args)


def place(y, z, core):
    return (y * NZ + z) * NC + core


def body(
    tiles,
    w_reduce,
    w_expand,
    att_tanh,
    att_gate,
    att_vector,
    classifier,
    tile_counts,
    target_weights,
):
    slots, positions, width = tiles.shape
    rows = slots * positions
    hid = w_reduce.shape[1]
    smem = pl.BlockSpec(memory_space=pltpu.SMEM)
    hbm = pl.BlockSpec(memory_space=pltpu.HBM)
    held = [
        pltpu.with_memory_space_constraint(x, pltpu.HBM)
        for x in (
            tiles.reshape(rows, width),
            w_reduce,
            w_expand,
            att_tanh,
            att_gate,
            att_vector.reshape(1, hid),
            classifier.T,
        )
    ]
    chunk = jax.ShapeDtypeStruct((CORE_NOTE + NOTE, 128), BF16)
    keep, send = call(
        local_kernel,
        (chunk, chunk),
        [smem] + [hbm] * 7,
        (tile_counts, *held),
        "local",
        [pltpu.VMEM((rows, width), BF16)]
        + [pltpu.VMEM((width, hid), BF16)] * 4
        + [pltpu.VMEM((1, hid), F32), pltpu.VMEM((2, width), F32)]
        + [pltpu.VMEM((rows, hid), BF16), pltpu.SemaphoreType.DMA((CHUNKS + 6,))],
    )
    everyone = [(y, z, c) for y in range(NY) for z in range(NZ) for c in range(NC)]

    def move(x, dy, dz, dc):
        pairs = [
            (place(y, z, c), place((y + dy) % NY, (z + dz) % NZ, (c + dc) % NC)) for y, z, c in everyone
        ]
        return lax.ppermute(x, "tile", pairs)

    def swap(x, away):
        return lax.ppermute(x, "tile", [(place(y, z, c), place(y, z ^ away[c], c)) for y, z, c in everyone])

    other = move(send, 0, 0, 1)
    piece = jax.ShapeDtypeStruct((Y_NOTE + NOTE, 128), BF16)
    pieces = call(core_kernel, (piece,) * NY, vmem(2), (keep, other), "join_cores")
    across = [move(pieces[2], 2, 0, 0), move(pieces[1], 1, 0, 0), move(pieces[3], 3, 0, 0)]
    piece = jax.ShapeDtypeStruct((PART + NOTE, 128), BF16)
    pieces = call(
        y_kernel,
        (piece,) * NZ,
        vmem(NY + 1),
        (pieces[0], *across, classifier.T),
        "join_y",
        [pltpu.VMEM((2 * PATH_ROWS, hid), BF16)],
    )
    across = [swap(pieces[k + 1], [away[k] for away in Z_AWAY]) for k in range(NZ - 1)]
    count = float(lax.axis_size("tile") * slots // 2)
    out = jax.ShapeDtypeStruct((ROWS, hid), F32)
    grad_w1, grad_w2, loss = call(
        functools.partial(z_kernel, count),
        (out, out, jax.ShapeDtypeStruct((1, 128), F32)),
        vmem(NZ) + [smem],
        (pieces[0], *across, target_weights),
        "join_z",
    )
    return grad_w1, grad_w2, loss[0, :1]


def solution(mesh):
    placed = (
        P(("slide", "tile"), None, None),
        P(),
        P(),
        P(),
        P(),
        P(),
        P(),
        P(("slide", "tile")),
        P("slide"),
    )
    return jax.shard_map(
        body,
        mesh=mesh,
        in_specs=placed,
        out_specs=(P(("slide", "tile"), None), P(("slide", "tile"), None), P("slide")),
        check_vma=False,
    )
```
